256 devices in a mesh: vocab: 64 (over z, y, core), rows: 4 (over x).
Axes of the slice: x: 4, y: 4, z: 8, core: 2. Of those that a mesh axis runs over, the one named last changes fastest.
Arguments:
- hidden: bfloat16 [2048, 2880], P('rows'), may hold values from -60 to 60, as said below
- head_weight: bfloat16 [2880, 106496], P(None, ('vocab', 'rows')), may hold values from -0.1118034 to 0.1118034, as said below
- eta_level: float32 [2048], P('rows'), may hold values from 0.0001 to 0.003
Outputs:
- filtered_log: float32 [2048, 106496], P('rows', 'vocab')
- entropy: float32 [2048], P('rows')
The draws below stay inside these ranges and needn't reach their ends.
Inputs may be any that keep to these rules, and one draw needn't show every extreme that they name: `hidden`: real-valued activations. `head_weight`: real-valued weights.
All inputs are finite; a program needn't handle non-finite values.
Results may differ from the reference program's by a relative error of at most 0.0003.
Values may be sent and summed in bfloat16 or wider, within the bound.
A program may use at most 64 MiB of HBM per device.

```python
import math
import jax
import jax.numpy as jnp
from jax import lax

D = 2880
VOCAB = 106496
ROWS = 2048


def column_block(key, block_id):
    block_key = jax.random.fold_in(jax.random.fold_in(key, 101), block_id)
    values = jax.random.normal(block_key, (128, D), jnp.float32) * D ** (-0.5)
    values = jnp.clip(values, -5.9 * D ** (-0.5), 5.9 * D ** (-0.5))
    return values.astype(jnp.bfloat16).astype(jnp.float32)


def draw_head_weight(key, part):
    block_ids = jnp.arange(VOCAB // 128, dtype=jnp.int32)
    blocks = jax.vmap(lambda block_id: column_block(key, block_id))(block_ids)
    return blocks.reshape(VOCAB, D).T.astype(jnp.bfloat16)


def draw_hidden(key, part):
    scale_key = jax.random.fold_in(key, 202)
    noise_key = jax.random.fold_in(key, 203)
    scales = jnp.exp(jax.random.uniform(scale_key, (ROWS, 1), jnp.float32, math.log(3.0), math.log(12.0)))
    values = jnp.clip(jax.random.normal(noise_key, (ROWS, D), jnp.float32), -4.0, 4.0) * scales
    return jnp.clip(values, -60.0, 60.0).astype(jnp.bfloat16)


def level_of(stream_key, extent, pieces, smallest, high):
    gain, own = 1.0, jax.random.fold_in(stream_key, 6)
    for dim, parts in pieces:
        steps = jnp.exp(jax.random.uniform(jax.random.fold_in(own, dim), (parts,), jnp.float32, smallest / len(pieces), high / len(pieces)))
        gain = gain * jnp.repeat(steps, extent[dim] // parts).reshape([-1 if axis == dim else 1 for axis in range(len(extent))])
    return gain


def setup_inputs(seed: int = 0) -> dict:
    keys = jax.random.split(jax.random.key(seed), 4)
    return {
        "hidden": draw_hidden(jax.random.fold_in(keys[3], 71), 0),
        "head_weight": draw_head_weight(jax.random.fold_in(keys[3], 71), 0),
        "eta_level": jnp.clip(jnp.exp(math.log(0.003) - 3.4011974 * jax.random.uniform(keys[2], (ROWS,), jnp.float32) ** level_of(keys[2], (ROWS,), ((0, 4),), -0.2, 0.2)), 0.0001, 0.003),
    }


def filter_block(inputs, head_weight):
    hidden_block, eta_block = inputs
    scores = jnp.dot(hidden_block, head_weight, preferred_element_type=jnp.float32)
    row_peak = lax.optimization_barrier(jnp.max(scores, axis=1, keepdims=True))
    shifted = jnp.exp(scores - row_peak)
    row_total = lax.optimization_barrier(jnp.sum(shifted, axis=1))
    moment = lax.optimization_barrier(jnp.sum(shifted * (scores - row_peak), axis=1))
    entropy = jnp.log(row_total) - moment / row_total
    threshold = jnp.minimum(eta_block, jnp.sqrt(eta_block) * jnp.exp(-entropy))
    row_probs = shifted / row_total[:, None]
    kept_weight = jnp.maximum(row_probs - threshold[:, None], 0.0)
    kept_mass = lax.optimization_barrier(jnp.sum(kept_weight, axis=1))
    filtered = jnp.log(kept_weight + 0.001 * threshold[:, None]) - jnp.log(kept_mass)[:, None]
    return (filtered, entropy)

def reference(hidden, head_weight, eta_level):
    block_rows = math.gcd(ROWS, 128)
    count_blocks = ROWS // block_rows
    hidden_blocks = hidden.reshape(count_blocks, block_rows, D)
    eta_blocks = eta_level.reshape(count_blocks, block_rows)
    filtered, entropy = lax.map(lambda inputs: filter_block(inputs, head_weight), (hidden_blocks, eta_blocks))
    return (filtered.reshape(ROWS, VOCAB), entropy.reshape(ROWS))
```

```python
import functools

import jax
import jax.numpy as jnp
from jax import lax
from jax.experimental import pallas as pl
from jax.experimental.pallas import tpu as pltpu
from jax.sharding import PartitionSpec as P

MESH = pl.DeviceIdType.MESH
F32 = jnp.float32
BF16 = jnp.bfloat16

NX, NY, NZ = 4, 4, 8
D = 2880
ROWS = 512
HALF = 256
PART = 128
COLS = 416
WIDE = 512
OUT = NX * COLS

LOG2E = 1.4426950408889634
LN2 = 0.6931471805599453
GAIN = 10.5
BIAS = 123.0
FLOOR = 23.5
NEG = -1e30


def far_first(n):
    return sorted(range(1, n), key=lambda k: -min(k, n - k))


def kernel(
    hid_hbm, w_hbm, eta_ref,
    log_hbm, lkm_ref, ent_ref,
    hid, wraw, wide, codes, stats, got, gstat, out,
    cols, part, zpart, ypart, kept, zkept, ykept,
    load_sem, send_sem, w_sem, x_sem, z_sem, y_sem, code_sem, stat_sem, round_sem, rsend_sem, out_sem,
):
    v = lax.axis_index("vocab")
    x = lax.axis_index("rows")
    z, y, c = v // 8, (v // 2) % 4, v % 2
    sg = 1 - 2 * c

    def at(z, y, c):
        return (z * NY + y) * 2 + c

    here = at(z, y, c)
    sibling = at(z, y, 1 - c)
    zto = [lax.rem(z + k, NZ) for k in range(NZ)]
    yto = [lax.rem(y + k, NY) for k in range(NY)]
    xto = [lax.rem(x + k, NX) for k in range(NX)]
    z_ahead = lax.rem(z + sg + NZ, NZ)
    z_back = lax.rem(z - sg + NZ, NZ)
    y_ahead = lax.rem(y + sg + NY, NY)
    y_back = lax.rem(y - sg + NY, NY)

    zpeers = [(at(zto[k], y, c), x) for k in far_first(NZ)]
    ypeers = [(at(z, yto[k], c), x) for k in (2,)]
    ypeers += [(at(z, yto[k], 1 - c), x) for k in (2, 1, 3)]
    ypeers += [(at(z, yto[k], c), x) for k in (1, 3)] + [(sibling, x)]
    xpeers = [(d, xto[k]) for k in (2, 1, 3) for d in (here, sibling)]

    own = pltpu.make_async_copy(
        hid_hbm.at[pl.ds(pl.multiple_of(HALF * c, HALF), HALF)], hid.at[0], load_sem.at[0])
    own.start()
    own_w = pltpu.make_async_copy(w_hbm, wraw.at[0], load_sem.at[1])
    own_w.start()

    barrier = pltpu.get_barrier_semaphore()
    peers = zpeers + ypeers + xpeers
    for peer in peers:
        pl.semaphore_signal(barrier, 1, device_id=peer, device_id_type=MESH)
    pl.semaphore_wait(barrier, len(peers))

    def y_rows(j):
        return pl.ds(pl.multiple_of(32 * j, 32), 32)

    def z_rows(j):
        return pl.ds(pl.multiple_of(PART + 16 * j, 16), 16)

    def x_send(s, g):
        if g:
            at_row, n = HALF * c + PART + 16 * z, 16
            to = hid.at[NX - s, z_rows(z)]
        else:
            at_row, n = HALF * c + 32 * y, 32
            to = hid.at[NX - s, y_rows(y)]
        pltpu.make_async_remote_copy(
            hid_hbm.at[pl.ds(pl.multiple_of(at_row, 16), n)], to,
            send_sem.at[0], x_sem.at[NX - s, g], device_id=(here, xto[s]), device_id_type=MESH,
        ).start()

    x_send(1, 1)
    x_send(3, 1)
    w_out = pltpu.make_async_remote_copy(
        w_hbm, wraw.at[1], send_sem.at[1], w_sem.at[0], device_id=(sibling, x), device_id_type=MESH)
    w_out.start()
    x_send(1, 0)
    x_send(3, 0)
    x_send(2, 1)
    x_send(2, 0)

    def await_rows(ref, sem):
        pltpu.make_async_copy(ref, ref, sem).wait()

    def z_send(s, j, step, ahead):
        ref = hid.at[s, z_rows(j)]
        pltpu.make_async_remote_copy(
            ref, ref, send_sem.at[0], z_sem.at[s, step, 0 if ahead else 1],
            device_id=(at(z_ahead if ahead else z_back, y, c), x), device_id_type=MESH,
        ).start()

    def y_send(s, j, step, ahead):
        ref = hid.at[s, y_rows(j)]
        pltpu.make_async_remote_copy(
            ref, ref, send_sem.at[0], y_sem.at[s, step, 0 if ahead else 1],
            device_id=(at(z, y_ahead if ahead else y_back, c), x), device_id_type=MESH,
        ).start()

    def z_step(s, t):
        if t == 0:
            await_rows(hid.at[s, z_rows(z)], x_sem.at[s, 1])
            z_send(s, z, 1, True)
            z_send(s, z, 1, False)
            return
        j = lax.rem(z - t * sg + NZ, NZ)
        await_rows(hid.at[s, z_rows(j)], z_sem.at[s, t, 0])
        if t < 4:
            z_send(s, j, t + 1, True)
            j = lax.rem(z + t * sg + NZ, NZ)
            await_rows(hid.at[s, z_rows(j)], z_sem.at[s, t, 1])
            if t < 3:
                z_send(s, j, t + 1, False)

    def y_step(s, t):
        if t == 0:
            await_rows(hid.at[s, y_rows(y)], x_sem.at[s, 0])
            y_send(s, y, 1, True)
            y_send(s, y, 1, False)
            return
        j = lax.rem(y - t * sg + NY, NY)
        await_rows(hid.at[s, y_rows(j)], y_sem.at[s, t, 0])
        if t < 2:
            y_send(s, j, t + 1, True)
            j = lax.rem(y + t * sg + NY, NY)
            await_rows(hid.at[s, y_rows(j)], y_sem.at[s, t, 1])

    rows_of = lax.broadcasted_iota(jnp.int32, (COLS, WIDE), 0)
    lanes_of = lax.broadcasted_iota(jnp.int32, (COLS, WIDE), 1)
    move = jnp.where(lanes_of == rows_of + 32 * x, 1.0, 0.0).astype(BF16)

    def spread(k):
        def body(i, _):
            rows = pl.ds(pl.multiple_of(i * 320, 320), 320)
            wide[rows, WIDE * k : WIDE * (k + 1)] = jnp.dot(
                wraw[k, rows, :], move, preferred_element_type=F32).astype(BF16)
            return 0
        lax.fori_loop(0, D // 320, body, 0)

    own_w.wait()
    cols[...] = jnp.zeros_like(cols)
    part[...] = jnp.zeros_like(part)
    kept[...] = jnp.zeros_like(kept)
    spread(0)
    z_step(1, 0)
    z_step(3, 0)
    y_step(1, 0)
    y_step(3, 0)
    w_out.wait_recv()
    spread(1)
    own.wait()

    plan = [
        [(z_step, 1, 1), (z_step, 3, 1), (z_step, 2, 0)],
        [(y_step, 2, 0), (z_step, 1, 2), (y_step, 1, 1), (y_step, 3, 1)],
        [(z_step, 3, 2), (z_step, 2, 1), (z_step, 1, 3), (y_step, 1, 2)],
        [(z_step, 3, 3), (z_step, 2, 2), (y_step, 2, 1), (z_step, 1, 4)],
        [(z_step, 2, 3), (y_step, 3, 2)],
        [(z_step, 3, 4)],
        [(y_step, 2, 2)],
        [(z_step, 2, 4)],
    ]
    lane = lax.broadcasted_iota(jnp.int32, (PART, WIDE), 1)
    valid = (lane >= 32 * x) & (lane < 32 * x + COLS)
    lane128 = lax.broadcasted_iota(jnp.int32, (PART, 128), 1)

    def chunk(i, _):
        for t, steps in enumerate(plan):
            @pl.when(i == t)
            def _():
                for step, s, n in steps:
                    step(s, n)

        j = i // 2
        g = i % 2
        s = j + jnp.where(j == 2, 1, 0) - jnp.where(j == 3, 1, 0)
        group = 2 * c + g
        block = hid[s, pl.ds(pl.multiple_of(PART * g, PART), PART), :]
        to_x = lax.rem(x + s, NX)
        from_s = lax.rem(NX - s, NX)
        for k in range(2):
            score = jnp.dot(block, wide[:, WIDE * k : WIDE * (k + 1)], preferred_element_type=F32)
            score = jnp.where(valid, score, NEG)
            peak = jnp.max(score, axis=1, keepdims=True)
            t = (score - peak) * LOG2E
            e = jnp.exp2(t)
            total = jnp.sum(e, axis=1, keepdims=True)
            moment = jnp.sum(e * t, axis=1, keepdims=True)
            code = jnp.exp2(jnp.maximum(t, -FLOOR) * GAIN + BIAS).astype(BF16)
            stat = jnp.where(lane128 == 0, peak, jnp.where(lane128 == 1, total, moment))
            stat = stat.T[0:8]
            codes[i, k] = code
            stats[i, k] = stat

            def send():
                pltpu.make_async_remote_copy(
                    codes.at[i, k], got.at[x, pl.ds(pl.multiple_of(PART * group, PART), PART)],
                    send_sem.at[2], code_sem.at[from_s, k, g],
                    device_id=(sibling if k else here, to_x), device_id_type=MESH,
                ).start()
                pltpu.make_async_remote_copy(
                    stats.at[i, k], gstat.at[x, group],
                    send_sem.at[3], stat_sem.at[from_s, k, g],
                    device_id=(sibling if k else here, to_x), device_id_type=MESH,
                ).start()

            if k == 0:
                @pl.when(i < 2)
                def _():
                    got[x, pl.ds(pl.multiple_of(PART * group, PART), PART), :] = code
                    gstat[x, group] = stat
                pl.when(i >= 2)(send)
            else:
                send()
        return 0

    lax.fori_loop(0, 8, chunk, 0)

    def await_group(ref_of, sem):
        for s in range(NX):
            for k in range(2):
                if s == 0 and k == 0:
                    continue
                for g in range(2):
                    ref = ref_of(xto[s], 2 * ((1 - c) if k else c) + g)
                    pltpu.make_async_copy(ref, ref, sem.at[s, k, g]).wait()

    await_group(lambda xs, group: gstat.at[xs, group], stat_sem)

    def combined(peaks, totals, moments):
        top = functools.reduce(jnp.maximum, peaks)
        total = moment = None
        for a, b, d in zip(peaks, totals, moments):
            low = (a - top) * LOG2E
            f = jnp.exp2(low)
            p, q = b * f, f * (d + low * b)
            total = p if total is None else total + p
            moment = q if moment is None else moment + q
        return top, total, moment

    def swap(mine, slots, place, peers, n):
        slots[place] = mine[...]
        for peer in peers:
            pltpu.make_async_remote_copy(
                mine, slots.at[place], rsend_sem.at[n], round_sem.at[n],
                device_id=peer, device_id_type=MESH,
            ).start()
        seven = slots.at[pl.ds(0, 7)]
        pltpu.make_async_copy(seven, seven, round_sem.at[n]).wait()
        pltpu.make_async_copy(seven, seven, rsend_sem.at[n]).wait()

    peaks = [gstat[k, :, 0, :] for k in range(NX)]
    top, total, moment = combined(
        peaks, [gstat[k, :, 1, :] for k in range(NX)], [gstat[k, :, 2, :] for k in range(NX)])
    yc = y * 2 + c
    for slots, place, peer_set, n in ((zpart, z, zpeers, 0), (ypart, yc, ypeers, 1)):
        part[0:4] = top
        part[4:8] = total
        part[8:12] = moment
        swap(part, slots, place, peer_set, n)
        top, total, moment = combined(
            [slots[k, 0:4] for k in range(8)], [slots[k, 4:8] for k in range(8)],
            [slots[k, 8:12] for k in range(8)])

    eta = eta_ref[...]
    entropy = jnp.log(total) - moment / total * LN2
    limit = jnp.minimum(eta, jnp.sqrt(eta) * jnp.exp(-entropy))
    ent_ref[...] = entropy
    under = jnp.log2(total) + BIAS / GAIN
    for k in range(NX):
        cols[:, k, :] = (peaks[k] - top) * LOG2E - under
    cols[:, NX, :] = limit

    await_group(lambda xs, group: got.at[xs, pl.ds(pl.multiple_of(PART * group, PART), PART)], code_sem)

    def finish(group, _):
        rows = pl.ds(pl.multiple_of(PART * group, PART), PART)
        col = cols[group].T
        shift = [col[:, k : k + 1] for k in range(NX)]
        cut = col[:, NX : NX + 1]
        least = 0.001 * cut
        acc = jnp.zeros((PART, 128), F32)
        for tile in range(OUT // 128):
            k = min(tile // 3, NX - 1)
            sent = got[k, rows, 128 * (tile - 3 * k) : 128 * (tile - 3 * k) + 128].astype(F32)
            off = shift[k]
            if tile % 3 == 0 and 0 < tile < 12:
                left = got[k - 1, rows, 384:512].astype(F32)
                sent = jnp.where(lane128 < 32 * k, left, sent)
                off = jnp.where(lane128 < 32 * k, shift[k - 1], shift[k])
            prob = jnp.exp2(jnp.log2(sent) * (1.0 / GAIN) + off)
            keep = jnp.maximum(prob - cut, 0.0)
            acc = acc + keep
            out[rows, 128 * tile : 128 * tile + 128] = jnp.log(keep + least)
        kept[pl.ds(group, 1)] = jnp.sum(acc.T, axis=0, keepdims=True)
        pltpu.make_async_copy(out.at[rows], log_hbm.at[rows], out_sem.at[group]).start()
        return 0

    lax.fori_loop(0, 4, finish, 0)

    for slots, place, peer_set, n in ((zkept, z, zpeers, 2), (ykept, yc, ypeers, 3)):
        swap(kept, slots, place, peer_set, n)
        mass = slots[0]
        for k in range(1, 8):
            mass = mass + slots[k]
        kept[...] = mass
    lkm_ref[...] = jnp.log(kept[0:4])

    for n, ref in ((0, hid.at[pl.ds(0, 3)]), (2, codes.at[pl.ds(0, 7)]), (3, stats.at[pl.ds(0, 7)])):
        pltpu.make_async_copy(ref, ref, send_sem.at[n]).wait()
    w_out.wait_send()
    for group in range(4):
        rows = pl.ds(PART * group, PART)
        pltpu.make_async_copy(out.at[rows], log_hbm.at[rows], out_sem.at[group]).wait()


def shards(hidden, head_weight, eta_level):
    dma = pltpu.SemaphoreType.DMA
    vmem = pltpu.VMEM
    logs, lkm, ent = pl.pallas_call(
        kernel,
        out_shape=(
            jax.ShapeDtypeStruct((ROWS, OUT), F32),
            jax.ShapeDtypeStruct((4, 128), F32),
            jax.ShapeDtypeStruct((4, 128), F32),
        ),
        in_specs=[
            pl.BlockSpec(memory_space=pl.ANY),
            pl.BlockSpec(memory_space=pl.ANY),
            pl.BlockSpec(memory_space=vmem),
        ],
        out_specs=(
            pl.BlockSpec(memory_space=pl.ANY),
            pl.BlockSpec(memory_space=vmem),
            pl.BlockSpec(memory_space=vmem),
        ),
        scratch_shapes=[
            vmem((NX, HALF, D), BF16),
            vmem((2, D, COLS), BF16),
            vmem((D, 2 * WIDE), BF16),
            vmem((8, 2, PART, WIDE), BF16),
            vmem((8, 2, 8, 128), F32),
            vmem((NX, ROWS, WIDE), BF16),
            vmem((NX, 4, 8, 128), F32),
            vmem((ROWS, OUT), F32),
            vmem((4, 128, 128), F32),
            vmem((16, 128), F32),
            vmem((8, 16, 128), F32),
            vmem((8, 16, 128), F32),
            vmem((8, 128), F32),
            vmem((8, 8, 128), F32),
            vmem((8, 8, 128), F32),
            dma((2,)),
            dma((4,)),
            dma((1,)),
            dma((NX, 2)),
            dma((NX, 5, 2)),
            dma((NX, 3, 2)),
            dma((NX, 2, 2)),
            dma((NX, 2, 2)),
            dma((4,)),
            dma((4,)),
            dma((4,)),
        ],
        compiler_params=pltpu.CompilerParams(
            collective_id=0, has_side_effects=True, vmem_limit_bytes=56 * 2**20),
        cost_estimate=pl.CostEstimate(
            flops=2 * ROWS * D * OUT, bytes_accessed=10 * 2**20, transcendentals=5 * ROWS * OUT),
        name="eta_filter",
    )(hidden, head_weight, eta_level.reshape(4, 128))
    return logs - lkm.reshape(ROWS)[:, None], ent.reshape(ROWS)


def solution(mesh):
    return jax.shard_map(
        shards,
        mesh=mesh,
        in_specs=(P("rows", None), P(None, ("vocab", "rows")), P("rows")),
        out_specs=(P("rows", "vocab"), P("rows")),
        check_vma=False,
    )
```

```python
import functools

import jax
import jax.numpy as jnp
from jax import lax
from jax.experimental import pallas as pl
from jax.experimental.pallas import tpu as pltpu
from jax.sharding import PartitionSpec as P

MESH = pl.DeviceIdType.MESH
F32 = jnp.float32
BF16 = jnp.bfloat16

NX, NY, NZ = 4, 4, 8
D = 2880
ROWS = 512
COLS = 416
OUT = NX * COLS
YPART = 432
ZPART = 144

LOG2E = 1.4426950408889634
LN2 = 0.6931471805599453
GAIN = 10.5
BIAS = 123.0
FLOOR = 23.5


def far_first(n):
    return sorted(range(1, n), key=lambda k: -min(k, n - k))


PLACE = {(1, 0): (1, 0), (3, 0): (1, 1), (1, 1): (2, 0), (3, 1): (2, 1), (2, 0): (3, 0), (2, 1): (3, 1)}


def kernel(
    hid_hbm, w_hbm, eta_ref,
    log_ref, lkm_ref, ent_ref,
    hid, w, codes, stats, got, gstat, keep,
    cols, part, zpart, ypart, kept, zkept, ykept,
    load_sem, send_sem, w_sem, x_sem, z_sem, y_sem, code_sem, stat_sem, round_sem, rsend_sem,
):
    v = lax.axis_index("vocab")
    x = lax.axis_index("rows")
    z, y, c = v // 8, (v // 2) % 4, v % 2
    sg = 1 - 2 * c

    def at(z, y, c):
        return (z * NY + y) * 2 + c

    here = at(z, y, c)
    sibling = at(z, y, 1 - c)
    zto = [lax.rem(z + k, NZ) for k in range(NZ)]
    yto = [lax.rem(y + k, NY) for k in range(NY)]
    xto = [lax.rem(x + k, NX) for k in range(NX)]
    x_ahead, x_back = lax.rem(x + sg + NX, NX), lax.rem(x - sg + NX, NX)
    y_ahead, y_back = lax.rem(y + sg + NY, NY), lax.rem(y - sg + NY, NY)
    z_ahead, z_back = lax.rem(z + sg + NZ, NZ), lax.rem(z - sg + NZ, NZ)

    zpeers = [(at(zto[k], y, c), x) for k in far_first(NZ)]
    ypeers = [(at(z, yto[2], c), x)]
    ypeers += [(at(z, yto[k], 1 - c), x) for k in (2, 1, 3)]
    ypeers += [(at(z, yto[k], c), x) for k in (1, 3)] + [(sibling, x)]
    xpeers = [(d, xto[k]) for k in (2, 1, 3) for d in (here, sibling)]

    barrier = pltpu.get_barrier_semaphore()
    peers = zpeers + ypeers + xpeers
    for peer in peers:
        pl.semaphore_signal(barrier, 1, device_id=peer, device_id_type=MESH)

    def lanes_of(lg):
        return pl.ds(pl.multiple_of(256 * c + 128 * lg, 128), 128)

    own = [
        pltpu.make_async_copy(hid_hbm.at[:, lanes_of(lg)], hid.at[0, lg], load_sem.at[lg])
        for lg in range(2)
    ]
    own.append(pltpu.make_async_copy(w_hbm, w.at[0], load_sem.at[2]))
    for copy in own:
        copy.start()
    part[...] = jnp.zeros_like(part)
    kept[...] = jnp.zeros_like(kept)
    pl.semaphore_wait(barrier, len(peers))

    def y_rows(j):
        return pl.ds(pl.multiple_of(YPART * j, 16), YPART)

    def z_rows(j):
        return pl.ds(pl.multiple_of(NY * YPART + ZPART * j, 16), ZPART)

    def hid_at(role, lg, rows):
        p, q = PLACE[role, lg]
        return hid.at[p, q, rows]

    def x_send(lg, along_z, ahead):
        rows = z_rows(z) if along_z else y_rows(y)
        role = 3 if ahead else 1
        pltpu.make_async_remote_copy(
            hid_hbm.at[rows, lanes_of(lg)], hid_at(role, lg, rows),
            send_sem.at[0], x_sem.at[role, lg, along_z],
            device_id=(here, x_ahead if ahead else x_back), device_id_type=MESH,
        ).start()

    x_send(1, 1, True)
    x_send(0, 1, True)
    x_send(1, 0, False)
    x_send(0, 1, False)
    w_out = pltpu.make_async_remote_copy(
        w_hbm, w.at[1], send_sem.at[1], w_sem.at[0], device_id=(sibling, x), device_id_type=MESH)
    w_out.start()
    x_send(1, 1, False)
    x_send(0, 0, False)
    x_send(0, 0, True)
    x_send(1, 0, True)

    def arrived(ref, sem):
        pltpu.make_async_copy(ref, ref, sem).wait()

    def pass_on(ref, sem, device):
        pltpu.make_async_remote_copy(
            ref, ref, send_sem.at[0], sem, device_id=device, device_id_type=MESH).start()

    def x_step(role, lg, along_z):
        rows = z_rows(z) if along_z else y_rows(y)
        ref = hid_at(role, lg, rows)
        arrived(ref, x_sem.at[role, lg, along_z])
        if role == (1 if along_z else 3):
            pltpu.make_async_remote_copy(
                ref, hid_at(2, lg, rows), send_sem.at[0], x_sem.at[2, lg, along_z],
                device_id=(here, x_back if along_z else x_ahead), device_id_type=MESH,
            ).start()

    def z_begin(role, lg):
        ref = hid_at(role, lg, z_rows(z))
        pass_on(ref, z_sem.at[role, lg, 1, 0], (at(z_ahead, y, c), x))
        pass_on(ref, z_sem.at[role, lg, 1, 1], (at(z_back, y, c), x))

    def z_step(role, lg, t, way):
        side = (1 - way) // 2
        ref = hid_at(role, lg, z_rows(lax.rem(z - way * t * sg + NZ, NZ)))
        arrived(ref, z_sem.at[role, lg, t, side])
        if t < (4, 3)[side]:
            pass_on(ref, z_sem.at[role, lg, t + 1, side], (at((z_ahead, z_back)[side], y, c), x))

    def y_begin(role, lg):
        ref = hid_at(role, lg, y_rows(y))
        pass_on(ref, y_sem.at[role, lg, 1, 0], (at(z, y_ahead, c), x))
        pass_on(ref, y_sem.at[role, lg, 1, 1], (at(z, y_back, c), x))

    def y_step(role, lg, t, way):
        side = (1 - way) // 2
        ref = hid_at(role, lg, y_rows(lax.rem(y - way * t * sg + NY, NY)))
        arrived(ref, y_sem.at[role, lg, t, side])
        if t < (2, 1)[side]:
            pass_on(ref, y_sem.at[role, lg, t + 1, side], (at(z, (y_ahead, y_back)[side], c), x))

    def own_here():
        for copy in own:
            copy.wait()

    plan = [
        [
            (own_here,),
        ],
        [
            (x_step, 3, 1, 1), (z_begin, 3, 1), (x_step, 3, 0, 1), (z_begin, 3, 0), (x_step, 1, 1, 0),
            (y_begin, 1, 1), (x_step, 1, 0, 1), (x_step, 1, 1, 1), (z_begin, 1, 0), (z_step, 3, 1, 1, 1),
            (x_step, 1, 0, 0), (y_begin, 1, 0), (z_step, 3, 0, 1, 1), (z_begin, 1, 1),
            (z_step, 3, 1, 1, -1), (x_step, 3, 0, 0), (y_begin, 3, 0), (z_step, 3, 0, 1, -1),
            (z_step, 1, 0, 1, 1), (x_step, 3, 1, 0), (x_step, 2, 0, 1), (z_begin, 2, 0), (x_step, 2, 1, 1),
            (z_step, 1, 0, 1, -1), (z_begin, 2, 1), (y_begin, 3, 1), (z_step, 3, 1, 2, 1),
            (w_out.wait_recv,), (z_step, 1, 1, 1, 1),
        ],
        [
            (z_step, 3, 0, 2, 1), (z_step, 1, 0, 2, 1), (y_step, 1, 0, 1, 1), (y_step, 1, 1, 1, -1),
            (z_step, 1, 1, 1, -1), (z_step, 3, 0, 2, -1), (x_step, 2, 1, 0), (y_step, 1, 0, 1, -1),
            (z_step, 2, 1, 1, 1), (z_step, 2, 0, 1, 1), (z_step, 3, 1, 2, -1), (x_step, 2, 0, 0),
            (z_step, 1, 1, 2, 1), (y_step, 3, 0, 1, 1), (z_step, 2, 1, 1, -1), (z_step, 1, 0, 2, -1),
            (z_step, 2, 0, 1, -1), (y_begin, 2, 0), (z_step, 3, 1, 3, 1), (z_step, 3, 0, 3, 1),
            (y_step, 1, 1, 1, 1), (z_step, 1, 0, 3, 1), (y_step, 3, 1, 1, -1), (y_step, 3, 0, 1, -1),
            (z_step, 2, 0, 2, 1), (z_step, 3, 1, 3, -1), (z_step, 1, 1, 2, -1), (y_step, 3, 1, 1, 1),
            (y_begin, 2, 1), (z_step, 1, 1, 3, 1), (y_step, 1, 0, 2, 1), (z_step, 1, 0, 3, -1),
            (z_step, 2, 1, 2, -1), (z_step, 3, 0, 3, -1), (z_step, 2, 0, 2, -1), (z_step, 2, 1, 2, 1),
            (y_step, 3, 0, 2, 1), (y_step, 2, 0, 1, 1), (z_step, 3, 0, 4, 1), (z_step, 1, 0, 4, 1),
        ],
        [
            (z_step, 2, 0, 3, 1), (z_step, 1, 1, 3, -1),
        ],
        [
            (y_step, 1, 1, 2, 1), (z_step, 1, 1, 4, 1), (y_step, 3, 1, 2, 1), (z_step, 3, 1, 4, 1),
            (z_step, 2, 1, 3, 1), (y_step, 2, 0, 1, -1), (y_step, 2, 1, 1, 1),
        ],
        [
            (z_step, 2, 0, 3, -1), (z_step, 2, 0, 4, 1),
        ],
        [
            (z_step, 2, 1, 3, -1), (y_step, 2, 0, 2, 1), (y_step, 2, 1, 1, -1), (z_step, 2, 1, 4, 1),
            (y_step, 2, 1, 2, 1),
        ],
        [],
    ]

    def chunk(i, _):
        for t, steps in enumerate(plan):
            @pl.when(i == t)
            def _():
                for step, *rest in steps:
                    step(*rest)

        p, k = i // 2, i % 2
        score = jnp.dot(
            w[k], jnp.concatenate([hid[p, 0], hid[p, 1]], axis=1), preferred_element_type=F32)
        peak = jnp.max(score, axis=0, keepdims=True)
        t = (score - peak) * LOG2E
        e = jnp.exp2(t)
        total = jnp.sum(e, axis=0, keepdims=True)
        moment = jnp.sum(e * t, axis=0, keepdims=True)
        code = jnp.exp2(jnp.maximum(t, -FLOOR) * GAIN + BIAS).astype(BF16)
        for q in range(2):
            lanes = slice(128 * q, 128 * q + 128)
            codes[i, q] = code[:, lanes]
            for n, row in enumerate((peak, total, moment)):
                stats[i, q, n : n + 1] = row[:, lanes]
        cols_here = pl.ds(pl.multiple_of(COLS * x, 16), COLS)

        @pl.when(i == 0)
        def _():
            for q in range(2):
                got[c, q, cols_here] = codes[i, q]
                gstat[x, 2 * c + q] = stats[i, q]

        def send(i, k, piece, land, sems, n):
            for q in range(2):
                role = jnp.where(p == 0, 0, jnp.where(p == 3, 2, 1 + 2 * q))
                lg = jnp.where((p == 0) | (p == 3), q, p - 1)
                device = (at(z, y, jnp.where(k == 1, 1 - c, c)), lax.rem(x + role * sg + NX, NX))
                pltpu.make_async_remote_copy(
                    piece.at[i, q], land(lg), send_sem.at[n], sems.at[x, c, lg],
                    device_id=device, device_id_type=MESH,
                ).start()

        def send_stats(i, k):
            send(i, k, stats, lambda lg: gstat.at[x, 2 * c + lg], stat_sem, 3)

        def send_codes(i, k):
            send(i, k, codes, lambda lg: got.at[c, lg, cols_here], code_sem, 2)

        @pl.when(i > 0)
        def _():
            send_stats(i, k)

        @pl.when((i > 0) & (i < 6))
        def _():
            send_codes(i, k)

        @pl.when(i == 7)
        def _():
            send_codes(6, 0)
            send_codes(7, 1)

        return 0

    lax.fori_loop(0, 8, chunk, 0)

    def await_groups(ref_of, sem):
        for s in range(NX):
            for h in ((1 - c,) if s == 0 else (c, 1 - c)):
                for lg in range(2):
                    ref = ref_of(xto[s], h, lg)
                    pltpu.make_async_copy(ref, ref, sem.at[xto[s], h, lg]).wait()

    await_groups(lambda xs, h, lg: gstat.at[xs, 2 * h + lg], stat_sem)

    def combined(peaks, totals, moments):
        top = functools.reduce(jnp.maximum, peaks)
        total = moment = None
        for a, b, d in zip(peaks, totals, moments):
            low = (a - top) * LOG2E
            f = jnp.exp2(low)
            m, n = b * f, f * (d + low * b)
            total = m if total is None else total + m
            moment = n if moment is None else moment + n
        return top, total, moment

    def swap_start(mine, slots, place, peers, n):
        slots[place] = mine[...]
        for peer in peers:
            pltpu.make_async_remote_copy(
                mine, slots.at[place], rsend_sem.at[n], round_sem.at[n],
                device_id=peer, device_id_type=MESH,
            ).start()

    def swap_end(slots, n):
        seven = slots.at[pl.ds(0, 7)]
        pltpu.make_async_copy(seven, seven, round_sem.at[n]).wait()
        pltpu.make_async_copy(seven, seven, rsend_sem.at[n]).wait()

    peaks = [gstat[k, :, 0, :] for k in range(NX)]
    top, total, moment = combined(
        peaks, [gstat[k, :, 1, :] for k in range(NX)], [gstat[k, :, 2, :] for k in range(NX)])
    yc = y * 2 + c
    for slots, place_at, peer_set, n in ((zpart, z, zpeers, 0), (ypart, yc, ypeers, 1)):
        part[0:4] = top
        part[4:8] = total
        part[8:12] = moment
        swap_start(part, slots, place_at, peer_set, n)
        swap_end(slots, n)
        top, total, moment = combined(
            [slots[k, 0:4] for k in range(8)], [slots[k, 4:8] for k in range(8)],
            [slots[k, 8:12] for k in range(8)])

    eta = eta_ref[...]
    entropy = jnp.log(total) - moment / total * LN2
    limit = jnp.minimum(eta, jnp.sqrt(eta) * jnp.exp(-entropy))
    ent_ref[...] = entropy
    under = jnp.log2(total) + BIAS / GAIN
    for k in range(NX):
        cols[:, k, :] = (peaks[k] - top) * LOG2E - under
    cols[:, NX, :] = limit

    await_groups(lambda xs, h, lg: got.at[h, lg, pl.ds(pl.multiple_of(COLS * xs, 16), COLS)], code_sem)

    def weigh(group, _):
        cut = cols[group, NX : NX + 1]
        mass = jnp.zeros((1, 128), F32)
        for k in range(NX):
            sent = got[group // 2, group % 2, COLS * k : COLS * (k + 1)].astype(F32)
            prob = jnp.exp2(jnp.log2(sent) * (1.0 / GAIN) + cols[group, k : k + 1])
            weight = jnp.maximum(prob - cut, 0.0)
            keep[group, COLS * k : COLS * (k + 1)] = weight
            mass = mass + jnp.sum(weight, axis=0, keepdims=True)
        kept[pl.ds(group, 1)] = mass
        return 0

    lax.fori_loop(0, 4, weigh, 0)

    def finish(group, _):
        least = 0.001 * cols[group, NX : NX + 1]
        rows = pl.ds(pl.multiple_of(128 * group, 128), 128)
        for tile in range(OUT // 128):
            at_tile = slice(128 * tile, 128 * tile + 128)
            log_ref[rows, at_tile] = jnp.log(keep[group, at_tile] + least).T
        return 0

    for slots, place_at, peer_set, n in ((zkept, z, zpeers, 2), (ykept, yc, ypeers, 3)):
        swap_start(kept, slots, place_at, peer_set, n)
        lax.fori_loop(2 * n - 4, 2 * n - 2, finish, 0)
        swap_end(slots, n)
        mass = slots[0]
        for k in range(1, 8):
            mass = mass + slots[k]
        kept[...] = mass
    lkm_ref[...] = jnp.log(kept[0:4])

    for n, ref in ((0, hid.at[pl.ds(0, 3)]), (2, codes.at[pl.ds(0, 7)]), (3, stats.at[pl.ds(0, 7)])):
        pltpu.make_async_copy(ref, ref, send_sem.at[n]).wait()
    w_out.wait_send()


def shards(hidden, head_weight, eta_level):
    dma = pltpu.SemaphoreType.DMA
    vmem = pltpu.VMEM
    logs, lkm, ent = pl.pallas_call(
        kernel,
        out_shape=(
            jax.ShapeDtypeStruct((ROWS, OUT), F32),
            jax.ShapeDtypeStruct((4, 128), F32),
            jax.ShapeDtypeStruct((4, 128), F32),
        ),
        in_specs=[
            pl.BlockSpec(memory_space=pltpu.HBM),
            pl.BlockSpec(memory_space=pltpu.HBM),
            pl.BlockSpec(memory_space=vmem),
        ],
        out_specs=(
            pl.BlockSpec(memory_space=vmem),
            pl.BlockSpec(memory_space=vmem),
            pl.BlockSpec(memory_space=vmem),
        ),
        scratch_shapes=[
            vmem((4, 2, D, 128), BF16),
            vmem((2, COLS, D), BF16),
            vmem((8, 2, COLS, 128), BF16),
            vmem((8, 2, 8, 128), F32),
            vmem((2, 2, OUT, 128), BF16),
            vmem((NX, 4, 8, 128), F32),
            vmem((4, OUT, 128), F32),
            vmem((4, 8, 128), F32),
            vmem((16, 128), F32),
            vmem((8, 16, 128), F32),
            vmem((8, 16, 128), F32),
            vmem((8, 128), F32),
            vmem((8, 8, 128), F32),
            vmem((8, 8, 128), F32),
            dma((3,)),
            dma((4,)),
            dma((1,)),
            dma((4, 2, 2)),
            dma((4, 2, 5, 2)),
            dma((4, 2, 3, 2)),
            dma((NX, 2, 2)),
            dma((NX, 2, 2)),
            dma((4,)),
            dma((4,)),
        ],
        compiler_params=pltpu.CompilerParams(
            collective_id=0, has_side_effects=True, vmem_limit_bytes=40 * 2**20),
        cost_estimate=pl.CostEstimate(
            flops=2 * ROWS * D * OUT, bytes_accessed=10 * 2**20, transcendentals=5 * ROWS * OUT),
        name="eta_filter",
    )(
        pltpu.with_memory_space_constraint(hidden.T, pltpu.HBM),
        pltpu.with_memory_space_constraint(head_weight.T, pltpu.HBM),
        eta_level.reshape(4, 128),
    )
    return logs - lkm.reshape(ROWS)[:, None], ent.reshape(ROWS)


def solution(mesh):
    return jax.shard_map(
        shards,
        mesh=mesh,
        in_specs=(P("rows", None), P(None, ("vocab", "rows")), P("rows")),
        out_specs=(P("rows", "vocab"), P("rows")),
        check_vma=False,
    )
```

```python
import functools

import jax
import jax.numpy as jnp
from jax import lax
from jax.experimental import pallas as pl
from jax.experimental.pallas import tpu as pltpu
from jax.sharding import PartitionSpec as P

MESH = pl.DeviceIdType.MESH
F32 = jnp.float32
BF16 = jnp.bfloat16

NX, NY, NZ = 4, 4, 8
D = 2880
ROWS = 512
COLS = 416
OUT = NX * COLS
YPART = 432
ZPART = 144

LOG2E = 1.4426950408889634
LN2 = 0.6931471805599453
GAIN = 10.5
BIAS = 123.0
FLOOR = 23.5


def far_first(n):
    return sorted(range(1, n), key=lambda k: -min(k, n - k))


PLACE = {(1, 0): (1, 0), (3, 0): (1, 1), (1, 1): (2, 0), (3, 1): (2, 1), (2, 0): (3, 0), (2, 1): (3, 1)}


def kernel(
    hid_hbm, w_hbm, eta_hbm,
    log_ref, lkm_ref, ent_ref,
    hid, w, eta_ref, codes, stats, got, gstat, keep,
    cols, part, zpart, ypart, kept, zkept, ykept,
    load_sem, send_sem, w_sem, x_sem, z_sem, y_sem, code_sem, stat_sem, round_sem, rsend_sem,
):
    v = lax.axis_index("vocab")
    x = lax.axis_index("rows")
    z, y, c = v // 8, (v // 2) % 4, v % 2
    sg = 1 - 2 * c

    def at(z, y, c):
        return (z * NY + y) * 2 + c

    here = at(z, y, c)
    sibling = at(z, y, 1 - c)
    zto = [lax.rem(z + k, NZ) for k in range(NZ)]
    yto = [lax.rem(y + k, NY) for k in range(NY)]
    xto = [lax.rem(x + k, NX) for k in range(NX)]
    x_ahead, x_back = lax.rem(x + sg + NX, NX), lax.rem(x - sg + NX, NX)
    y_ahead, y_back = lax.rem(y + sg + NY, NY), lax.rem(y - sg + NY, NY)
    z_ahead, z_back = lax.rem(z + sg + NZ, NZ), lax.rem(z - sg + NZ, NZ)

    zpeers = [(at(zto[k], y, c), x) for k in far_first(NZ)]
    ypeers = [(at(z, yto[2], c), x)]
    ypeers += [(at(z, yto[k], 1 - c), x) for k in (2, 1, 3)]
    ypeers += [(at(z, yto[k], c), x) for k in (1, 3)] + [(sibling, x)]
    xpeers = [(d, xto[k]) for k in (2, 1, 3) for d in (here, sibling)]

    barrier = pltpu.get_barrier_semaphore()
    peers = zpeers + ypeers + xpeers
    for peer in peers:
        pl.semaphore_signal(barrier, 1, device_id=peer, device_id_type=MESH)

    def lanes_of(lg):
        return pl.ds(pl.multiple_of(256 * c + 128 * lg, 128), 128)

    own = [
        pltpu.make_async_copy(hid_hbm.at[:, lanes_of(lg)], hid.at[0, lg], load_sem.at[lg])
        for lg in range(2)
    ]
    own.append(pltpu.make_async_copy(w_hbm, w.at[0], load_sem.at[2]))
    own.append(pltpu.make_async_copy(eta_hbm, eta_ref, load_sem.at[3]))
    for copy in own:
        copy.start()
    part[...] = jnp.zeros_like(part)
    kept[...] = jnp.zeros_like(kept)
    pl.semaphore_wait(barrier, len(peers))

    def y_rows(j):
        return pl.ds(pl.multiple_of(YPART * j, 16), YPART)

    def z_rows(j):
        return pl.ds(pl.multiple_of(NY * YPART + ZPART * j, 16), ZPART)

    def hid_at(role, lg, rows):
        p, q = PLACE[role, lg]
        return hid.at[p, q, rows]

    def x_send(lg, along_z, ahead):
        rows = z_rows(z) if along_z else y_rows(y)
        role = 3 if ahead else 1
        pltpu.make_async_remote_copy(
            hid_hbm.at[rows, lanes_of(lg)], hid_at(role, lg, rows),
            send_sem.at[0], x_sem.at[role, lg, along_z],
            device_id=(here, x_ahead if ahead else x_back), device_id_type=MESH,
        ).start()

    x_send(1, 1, True)
    x_send(0, 1, True)
    x_send(1, 0, False)
    x_send(0, 1, False)
    w_out = pltpu.make_async_remote_copy(
        w_hbm, w.at[1], send_sem.at[1], w_sem.at[0], device_id=(sibling, x), device_id_type=MESH)
    w_out.start()
    x_send(1, 1, False)
    x_send(0, 0, False)
    x_send(0, 0, True)
    x_send(1, 0, True)

    def arrived(ref, sem):
        pltpu.make_async_copy(ref, ref, sem).wait()

    def pass_on(ref, sem, device):
        pltpu.make_async_remote_copy(
            ref, ref, send_sem.at[0], sem, device_id=device, device_id_type=MESH).start()

    def x_step(role, lg, along_z):
        rows = z_rows(z) if along_z else y_rows(y)
        ref = hid_at(role, lg, rows)
        arrived(ref, x_sem.at[role, lg, along_z])
        if role == (1 if along_z else 3):
            pltpu.make_async_remote_copy(
                ref, hid_at(2, lg, rows), send_sem.at[0], x_sem.at[2, lg, along_z],
                device_id=(here, x_back if along_z else x_ahead), device_id_type=MESH,
            ).start()

    def z_begin(role, lg):
        ref = hid_at(role, lg, z_rows(z))
        pass_on(ref, z_sem.at[role, lg, 1, 0], (at(z_ahead, y, c), x))
        pass_on(ref, z_sem.at[role, lg, 1, 1], (at(z_back, y, c), x))

    def z_step(role, lg, t, way):
        side = (1 - way) // 2
        ref = hid_at(role, lg, z_rows(lax.rem(z - way * t * sg + NZ, NZ)))
        arrived(ref, z_sem.at[role, lg, t, side])
        if t < (4, 3)[side]:
            pass_on(ref, z_sem.at[role, lg, t + 1, side], (at((z_ahead, z_back)[side], y, c), x))

    def y_begin(role, lg):
        ref = hid_at(role, lg, y_rows(y))
        pass_on(ref, y_sem.at[role, lg, 1, 0], (at(z, y_ahead, c), x))
        pass_on(ref, y_sem.at[role, lg, 1, 1], (at(z, y_back, c), x))

    def y_step(role, lg, t, way):
        side = (1 - way) // 2
        ref = hid_at(role, lg, y_rows(lax.rem(y - way * t * sg + NY, NY)))
        arrived(ref, y_sem.at[role, lg, t, side])
        if t < (2, 1)[side]:
            pass_on(ref, y_sem.at[role, lg, t + 1, side], (at(z, (y_ahead, y_back)[side], c), x))

    def own_here():
        for copy in own:
            copy.wait()

    plan = [
        [
            (own_here,),
        ],
        [
            (x_step, 3, 1, 1), (z_begin, 3, 1), (x_step, 3, 0, 1), (z_begin, 3, 0), (x_step, 1, 1, 0),
            (y_begin, 1, 1), (x_step, 1, 0, 1), (x_step, 1, 1, 1), (z_begin, 1, 0), (z_step, 3, 1, 1, 1),
            (x_step, 1, 0, 0), (y_begin, 1, 0), (z_step, 3, 0, 1, 1), (z_begin, 1, 1),
            (z_step, 3, 1, 1, -1), (x_step, 3, 0, 0), (y_begin, 3, 0), (z_step, 3, 0, 1, -1),
            (z_step, 1, 0, 1, 1), (x_step, 3, 1, 0), (x_step, 2, 0, 1), (z_begin, 2, 0), (x_step, 2, 1, 1),
            (z_step, 1, 0, 1, -1), (z_begin, 2, 1), (y_begin, 3, 1), (z_step, 3, 1, 2, 1),
            (w_out.wait_recv,), (z_step, 1, 1, 1, 1),
        ],
        [
            (z_step, 3, 0, 2, 1), (z_step, 1, 0, 2, 1), (y_step, 1, 0, 1, 1), (y_step, 1, 1, 1, -1),
            (z_step, 1, 1, 1, -1), (z_step, 3, 0, 2, -1), (x_step, 2, 1, 0), (y_step, 1, 0, 1, -1),
            (z_step, 2, 1, 1, 1), (z_step, 2, 0, 1, 1), (z_step, 3, 1, 2, -1), (x_step, 2, 0, 0),
            (z_step, 1, 1, 2, 1), (y_step, 3, 0, 1, 1), (z_step, 2, 1, 1, -1), (z_step, 1, 0, 2, -1),
            (z_step, 2, 0, 1, -1), (y_begin, 2, 0), (z_step, 3, 1, 3, 1), (z_step, 3, 0, 3, 1),
            (y_step, 1, 1, 1, 1), (z_step, 1, 0, 3, 1), (y_step, 3, 1, 1, -1), (y_step, 3, 0, 1, -1),
            (z_step, 2, 0, 2, 1), (z_step, 3, 1, 3, -1), (z_step, 1, 1, 2, -1), (y_step, 3, 1, 1, 1),
            (y_begin, 2, 1), (z_step, 1, 1, 3, 1), (y_step, 1, 0, 2, 1), (z_step, 1, 0, 3, -1),
            (z_step, 2, 1, 2, -1), (z_step, 3, 0, 3, -1), (z_step, 2, 0, 2, -1), (z_step, 2, 1, 2, 1),
            (y_step, 3, 0, 2, 1), (y_step, 2, 0, 1, 1), (z_step, 3, 0, 4, 1), (z_step, 1, 0, 4, 1),
        ],
        [
            (z_step, 2, 0, 3, 1), (z_step, 1, 1, 3, -1),
        ],
        [
            (y_step, 1, 1, 2, 1), (z_step, 1, 1, 4, 1), (y_step, 3, 1, 2, 1), (z_step, 3, 1, 4, 1),
            (z_step, 2, 1, 3, 1), (y_step, 2, 0, 1, -1), (y_step, 2, 1, 1, 1),
        ],
        [
            (z_step, 2, 0, 3, -1), (z_step, 2, 0, 4, 1),
        ],
        [
            (z_step, 2, 1, 3, -1), (y_step, 2, 0, 2, 1), (y_step, 2, 1, 1, -1), (z_step, 2, 1, 4, 1),
            (y_step, 2, 1, 2, 1),
        ],
        [],
    ]

    def chunk(i, _):
        for t, steps in enumerate(plan):
            @pl.when(i == t)
            def _():
                for step, *rest in steps:
                    step(*rest)

        p, k = i // 2, i % 2
        score = jnp.dot(
            w[k], jnp.concatenate([hid[p, 0], hid[p, 1]], axis=1), preferred_element_type=F32)
        peak = jnp.max(score, axis=0, keepdims=True)
        t = (score - peak) * LOG2E
        e = jnp.exp2(t)
        total = jnp.sum(e, axis=0, keepdims=True)
        moment = jnp.sum(e * t, axis=0, keepdims=True)
        code = jnp.exp2(jnp.maximum(t, -FLOOR) * GAIN + BIAS).astype(BF16)
        for q in range(2):
            lanes = slice(128 * q, 128 * q + 128)
            codes[i, q] = code[:, lanes]
            for n, row in enumerate((peak, total, moment)):
                stats[i, q, n : n + 1] = row[:, lanes]
        cols_here = pl.ds(pl.multiple_of(COLS * x, 16), COLS)

        @pl.when(i == 0)
        def _():
            for q in range(2):
                got[c, q, cols_here] = codes[i, q]
                gstat[x, 2 * c + q] = stats[i, q]

        def send(i, k, piece, land, sems, n):
            for q in range(2):
                role = jnp.where(p == 0, 0, jnp.where(p == 3, 2, 1 + 2 * q))
                lg = jnp.where((p == 0) | (p == 3), q, p - 1)
                device = (at(z, y, jnp.where(k == 1, 1 - c, c)), lax.rem(x + role * sg + NX, NX))
                pltpu.make_async_remote_copy(
                    piece.at[i, q], land(lg), send_sem.at[n], sems.at[x, c, lg],
                    device_id=device, device_id_type=MESH,
                ).start()

        def send_stats(i, k):
            send(i, k, stats, lambda lg: gstat.at[x, 2 * c + lg], stat_sem, 3)

        def send_codes(i, k):
            send(i, k, codes, lambda lg: got.at[c, lg, cols_here], code_sem, 2)

        @pl.when(i > 0)
        def _():
            send_stats(i, k)

        @pl.when((i > 0) & (i < 6))
        def _():
            send_codes(i, k)

        @pl.when(i == 7)
        def _():
            send_codes(6, 0)
            send_codes(7, 1)

        return 0

    lax.fori_loop(0, 8, chunk, 0)

    def await_groups(ref_of, sem):
        for s in range(NX):
            for h in ((1 - c,) if s == 0 else (c, 1 - c)):
                for lg in range(2):
                    ref = ref_of(xto[s], h, lg)
                    pltpu.make_async_copy(ref, ref, sem.at[xto[s], h, lg]).wait()

    await_groups(lambda xs, h, lg: gstat.at[xs, 2 * h + lg], stat_sem)

    def combined(peaks, totals, moments):
        top = functools.reduce(jnp.maximum, peaks)
        total = moment = None
        for a, b, d in zip(peaks, totals, moments):
            low = (a - top) * LOG2E
            f = jnp.exp2(low)
            m, n = b * f, f * (d + low * b)
            total = m if total is None else total + m
            moment = n if moment is None else moment + n
        return top, total, moment

    def swap_start(mine, slots, place, peers, n):
        slots[place] = mine[...]
        for peer in peers:
            pltpu.make_async_remote_copy(
                mine, slots.at[place], rsend_sem.at[n], round_sem.at[n],
                device_id=peer, device_id_type=MESH,
            ).start()

    def swap_end(slots, n):
        seven = slots.at[pl.ds(0, 7)]
        pltpu.make_async_copy(seven, seven, round_sem.at[n]).wait()
        pltpu.make_async_copy(seven, seven, rsend_sem.at[n]).wait()

    peaks = [gstat[k, :, 0, :] for k in range(NX)]
    top, total, moment = combined(
        peaks, [gstat[k, :, 1, :] for k in range(NX)], [gstat[k, :, 2, :] for k in range(NX)])
    yc = y * 2 + c
    for slots, place_at, peer_set, n in ((zpart, z, zpeers, 0), (ypart, yc, ypeers, 1)):
        part[0:4] = top
        part[4:8] = total
        part[8:12] = moment
        swap_start(part, slots, place_at, peer_set, n)
        swap_end(slots, n)
        top, total, moment = combined(
            [slots[k, 0:4] for k in range(8)], [slots[k, 4:8] for k in range(8)],
            [slots[k, 8:12] for k in range(8)])

    eta = eta_ref[...]
    entropy = jnp.log(total) - moment / total * LN2
    limit = jnp.minimum(eta, jnp.sqrt(eta) * jnp.exp(-entropy))
    ent_ref[...] = entropy
    under = jnp.log2(total) + BIAS / GAIN
    for k in range(NX):
        cols[:, k, :] = (peaks[k] - top) * LOG2E - under
    cols[:, NX, :] = limit

    def await_codes(s):
        cols_from = pl.ds(pl.multiple_of(COLS * xto[s], 16), COLS)
        for h in ((1 - c,) if s == 0 else (c, 1 - c)):
            for lg in range(2):
                ref = got.at[h, lg, cols_from]
                pltpu.make_async_copy(ref, ref, code_sem.at[xto[s], h, lg]).wait()

    def weigh(group, sources):
        cut = cols[group, NX : NX + 1]
        mass = jnp.zeros((1, 128), F32)
        for s in sources:
            cols_from = pl.ds(pl.multiple_of(COLS * xto[s], 16), COLS)
            sent = got[group // 2, group % 2, cols_from].astype(F32)
            prob = jnp.exp2(jnp.log2(sent) * (1.0 / GAIN) + cols[group, pl.ds(xto[s], 1)])
            weight = jnp.maximum(prob - cut, 0.0)
            keep[group, cols_from] = weight
            mass = mass + jnp.sum(weight, axis=0, keepdims=True)
        kept[pl.ds(group, 1)] = kept[pl.ds(group, 1)] + mass

    for sources in ((0, 1, 3), (2,)):
        for s in sources:
            await_codes(s)

        def weigh_group(group, _, sources=sources):
            weigh(group, sources)
            return 0
        lax.fori_loop(0, 4, weigh_group, 0)

    def finish(group, _):
        least = 0.001 * cols[group, NX : NX + 1]
        rows = pl.ds(pl.multiple_of(128 * group, 128), 128)
        for tile in range(OUT // 128):
            at_tile = slice(128 * tile, 128 * tile + 128)
            log_ref[rows, at_tile] = jnp.log(keep[group, at_tile] + least).T
        return 0

    for slots, place_at, peer_set, n in ((zkept, z, zpeers, 2), (ykept, yc, ypeers, 3)):
        swap_start(kept, slots, place_at, peer_set, n)
        lax.fori_loop(2 * n - 4, 2 * n - 2, finish, 0)
        swap_end(slots, n)
        mass = slots[0]
        for k in range(1, 8):
            mass = mass + slots[k]
        kept[...] = mass
    lkm_ref[...] = jnp.log(kept[0:4])

    for n, ref in ((0, hid.at[pl.ds(0, 3)]), (2, codes.at[pl.ds(0, 7)]), (3, stats.at[pl.ds(0, 7)])):
        pltpu.make_async_copy(ref, ref, send_sem.at[n]).wait()
    w_out.wait_send()


def write_out(log_ref, lkm_ref, ent_ref, out_hbm, ent_out, out, sem):
    copies = []
    for group in range(4):
        rows = slice(128 * group, 128 * group + 128)
        less = jnp.broadcast_to(lkm_ref[group : group + 1], (128, 128)).T
        for tile in range(OUT // 128):
            at_tile = slice(128 * tile, 128 * tile + 128)
            out[group, :, at_tile] = log_ref[rows, at_tile] - less
        copies.append(pltpu.make_async_copy(out.at[group], out_hbm.at[rows], sem.at[group]))
        copies[-1].start()
    ent_out[...] = ent_ref[...]
    for copy in copies:
        copy.wait()


def shards(hidden, head_weight, eta_level):
    dma = pltpu.SemaphoreType.DMA
    vmem = pltpu.VMEM
    logs, lkm, ent = pl.pallas_call(
        kernel,
        out_shape=(
            jax.ShapeDtypeStruct((ROWS, OUT), F32),
            jax.ShapeDtypeStruct((4, 128), F32),
            jax.ShapeDtypeStruct((4, 128), F32),
        ),
        in_specs=[
            pl.BlockSpec(memory_space=pltpu.HBM),
            pl.BlockSpec(memory_space=pltpu.HBM),
            pl.BlockSpec(memory_space=pltpu.HBM),
        ],
        out_specs=(
            pl.BlockSpec(memory_space=vmem),
            pl.BlockSpec(memory_space=vmem),
            pl.BlockSpec(memory_space=vmem),
        ),
        scratch_shapes=[
            vmem((4, 2, D, 128), BF16),
            vmem((2, COLS, D), BF16),
            vmem((4, 128), F32),
            vmem((8, 2, COLS, 128), BF16),
            vmem((8, 2, 8, 128), F32),
            vmem((2, 2, OUT, 128), BF16),
            vmem((NX, 4, 8, 128), F32),
            vmem((4, OUT, 128), F32),
            vmem((4, 8, 128), F32),
            vmem((16, 128), F32),
            vmem((8, 16, 128), F32),
            vmem((8, 16, 128), F32),
            vmem((8, 128), F32),
            vmem((8, 8, 128), F32),
            vmem((8, 8, 128), F32),
            dma((4,)),
            dma((4,)),
            dma((1,)),
            dma((4, 2, 2)),
            dma((4, 2, 5, 2)),
            dma((4, 2, 3, 2)),
            dma((NX, 2, 2)),
            dma((NX, 2, 2)),
            dma((4,)),
            dma((4,)),
        ],
        compiler_params=pltpu.CompilerParams(
            collective_id=0, has_side_effects=True, vmem_limit_bytes=40 * 2**20),
        cost_estimate=pl.CostEstimate(
            flops=2 * ROWS * D * OUT, bytes_accessed=10 * 2**20, transcendentals=5 * ROWS * OUT),
        name="eta_filter",
    )(
        pltpu.with_memory_space_constraint(hidden.T, pltpu.HBM),
        pltpu.with_memory_space_constraint(head_weight.T, pltpu.HBM),
        pltpu.with_memory_space_constraint(eta_level.reshape(4, 128), pltpu.HBM),
    )
    filtered, entropy = pl.pallas_call(
        write_out,
        out_shape=(jax.ShapeDtypeStruct((ROWS, OUT), F32), jax.ShapeDtypeStruct((4, 128), F32)),
        in_specs=[pl.BlockSpec(memory_space=vmem)] * 3,
        out_specs=(pl.BlockSpec(memory_space=pltpu.HBM), pl.BlockSpec(memory_space=vmem)),
        scratch_shapes=[vmem((4, 128, OUT), F32), dma((4,))],
        compiler_params=pltpu.CompilerParams(vmem_limit_bytes=16 * 2**20),
        cost_estimate=pl.CostEstimate(flops=ROWS * OUT, bytes_accessed=4 * ROWS * OUT, transcendentals=0),
        name="write_out",
    )(pltpu.with_memory_space_constraint(logs, vmem), lkm, ent)
    return filtered, entropy.reshape(ROWS)


def solution(mesh):
    return jax.shard_map(
        shards,
        mesh=mesh,
        in_specs=(P("rows", None), P(None, ("vocab", "rows")), P("rows")),
        out_specs=(P("rows", "vocab"), P("rows")),
        check_vma=False,
    )
```

```python
import functools

import jax
import jax.numpy as jnp
from jax import lax
from jax.experimental import pallas as pl
from jax.experimental.pallas import tpu as pltpu
from jax.sharding import PartitionSpec as P

MESH = pl.DeviceIdType.MESH
F32 = jnp.float32
BF16 = jnp.bfloat16

NX, NY, NZ = 4, 4, 8
D = 2880
ROWS = 512
COLS = 416
OUT = NX * COLS
YPART = 432
ZPART = 144

LOG2E = 1.4426950408889634
LN2 = 0.6931471805599453
GAIN = 10.5
BIAS = 123.0
FLOOR = 23.5


def far_first(n):
    return sorted(range(1, n), key=lambda k: -min(k, n - k))


PLACE = {(1, 0): (1, 0), (3, 0): (1, 1), (1, 1): (2, 0), (3, 1): (2, 1), (2, 0): (3, 0), (2, 1): (3, 1)}


def kernel(
    hid_hbm, w_hbm, eta_hbm,
    log_ref, lkm_ref, ent_ref,
    hid, w, eta_ref, codes, stats, got, gstat, keep,
    cols, part, zpart, ypart, kept, zkept, ykept,
    load_sem, send_sem, w_sem, x_sem, z_sem, y_sem, code_sem, stat_sem, round_sem, rsend_sem,
):
    v = lax.axis_index("vocab")
    x = lax.axis_index("rows")
    z, y, c = v // 8, (v // 2) % 4, v % 2
    sg = 1 - 2 * c

    def at(z, y, c):
        return (z * NY + y) * 2 + c

    here = at(z, y, c)
    sibling = at(z, y, 1 - c)
    zto = [lax.rem(z + k, NZ) for k in range(NZ)]
    yto = [lax.rem(y + k, NY) for k in range(NY)]
    xto = [lax.rem(x + k, NX) for k in range(NX)]
    x_ahead, x_back = lax.rem(x + sg + NX, NX), lax.rem(x - sg + NX, NX)
    y_ahead, y_back = lax.rem(y + sg + NY, NY), lax.rem(y - sg + NY, NY)
    z_ahead, z_back = lax.rem(z + sg + NZ, NZ), lax.rem(z - sg + NZ, NZ)

    zpeers = [(at(zto[k], y, c), x) for k in far_first(NZ)]
    ypeers = [(at(z, yto[2], c), x)]
    ypeers += [(at(z, yto[k], 1 - c), x) for k in (2, 1, 3)]
    ypeers += [(at(z, yto[k], c), x) for k in (1, 3)] + [(sibling, x)]
    xpeers = [(d, xto[k]) for k in (2, 1, 3) for d in (here, sibling)]

    barrier = pltpu.get_barrier_semaphore()
    peers = zpeers + ypeers + xpeers
    for peer in peers:
        pl.semaphore_signal(barrier, 1, device_id=peer, device_id_type=MESH)

    def lanes_of(lg):
        return pl.ds(pl.multiple_of(256 * c + 128 * lg, 128), 128)

    own = [
        pltpu.make_async_copy(hid_hbm.at[:, lanes_of(lg)], hid.at[0, lg], load_sem.at[lg])
        for lg in range(2)
    ]
    own.append(pltpu.make_async_copy(w_hbm, w.at[0], load_sem.at[2]))
    own.append(pltpu.make_async_copy(eta_hbm, eta_ref, load_sem.at[3]))
    for copy in own:
        copy.start()
    part[...] = jnp.zeros_like(part)
    kept[...] = jnp.zeros_like(kept)
    pl.semaphore_wait(barrier, len(peers))

    def y_rows(j):
        return pl.ds(pl.multiple_of(YPART * j, 16), YPART)

    def z_rows(j):
        return pl.ds(pl.multiple_of(NY * YPART + ZPART * j, 16), ZPART)

    def hid_at(role, lg, rows):
        p, q = PLACE[role, lg]
        return hid.at[p, q, rows]

    def x_send(lg, along_z, ahead):
        rows = z_rows(z) if along_z else y_rows(y)
        role = 3 if ahead else 1
        pltpu.make_async_remote_copy(
            hid_hbm.at[rows, lanes_of(lg)], hid_at(role, lg, rows),
            send_sem.at[0], x_sem.at[role, lg, along_z],
            device_id=(here, x_ahead if ahead else x_back), device_id_type=MESH,
        ).start()

    x_send(1, 1, True)
    x_send(0, 1, True)
    x_send(1, 0, False)
    x_send(0, 1, False)
    w_out = pltpu.make_async_remote_copy(
        w_hbm, w.at[1], send_sem.at[1], w_sem.at[0], device_id=(sibling, x), device_id_type=MESH)
    w_out.start()
    x_send(1, 1, False)
    x_send(0, 0, False)
    x_send(0, 0, True)
    x_send(1, 0, True)

    def arrived(ref, sem):
        pltpu.make_async_copy(ref, ref, sem).wait()

    def pass_on(ref, sem, device):
        pltpu.make_async_remote_copy(
            ref, ref, send_sem.at[0], sem, device_id=device, device_id_type=MESH).start()

    def x_step(role, lg, along_z):
        rows = z_rows(z) if along_z else y_rows(y)
        ref = hid_at(role, lg, rows)
        arrived(ref, x_sem.at[role, lg, along_z])
        if role == (1 if along_z else 3):
            pltpu.make_async_remote_copy(
                ref, hid_at(2, lg, rows), send_sem.at[0], x_sem.at[2, lg, along_z],
                device_id=(here, x_back if along_z else x_ahead), device_id_type=MESH,
            ).start()

    def z_begin(role, lg):
        ref = hid_at(role, lg, z_rows(z))
        pass_on(ref, z_sem.at[role, lg, 1, 0], (at(z_ahead, y, c), x))
        pass_on(ref, z_sem.at[role, lg, 1, 1], (at(z_back, y, c), x))

    def z_step(role, lg, t, way):
        side = (1 - way) // 2
        ref = hid_at(role, lg, z_rows(lax.rem(z - way * t * sg + NZ, NZ)))
        arrived(ref, z_sem.at[role, lg, t, side])
        if t < (4, 3)[side]:
            pass_on(ref, z_sem.at[role, lg, t + 1, side], (at((z_ahead, z_back)[side], y, c), x))

    def y_begin(role, lg):
        ref = hid_at(role, lg, y_rows(y))
        pass_on(ref, y_sem.at[role, lg, 1, 0], (at(z, y_ahead, c), x))
        pass_on(ref, y_sem.at[role, lg, 1, 1], (at(z, y_back, c), x))

    def y_step(role, lg, t, way):
        side = (1 - way) // 2
        ref = hid_at(role, lg, y_rows(lax.rem(y - way * t * sg + NY, NY)))
        arrived(ref, y_sem.at[role, lg, t, side])
        if t < (2, 1)[side]:
            pass_on(ref, y_sem.at[role, lg, t + 1, side], (at(z, (y_ahead, y_back)[side], c), x))

    def own_here():
        for copy in own:
            copy.wait()

    plan = [
        [
            (own_here,),
        ],
        [
            (x_step, 3, 1, 1), (z_begin, 3, 1), (x_step, 3, 0, 1), (z_begin, 3, 0), (x_step, 1, 1, 0),
            (y_begin, 1, 1), (x_step, 1, 0, 1), (x_step, 1, 1, 1), (z_begin, 1, 0), (z_step, 3, 1, 1, 1),
            (x_step, 1, 0, 0), (y_begin, 1, 0), (z_step, 3, 0, 1, 1), (z_begin, 1, 1),
            (z_step, 3, 1, 1, -1), (x_step, 3, 0, 0), (y_begin, 3, 0), (z_step, 3, 0, 1, -1),
            (z_step, 1, 0, 1, 1), (x_step, 3, 1, 0), (x_step, 2, 0, 1), (z_begin, 2, 0), (x_step, 2, 1, 1),
            (z_step, 1, 0, 1, -1), (z_begin, 2, 1), (y_begin, 3, 1), (z_step, 3, 1, 2, 1),
            (w_out.wait_recv,), (z_step, 1, 1, 1, 1),
        ],
        [
            (z_step, 3, 0, 2, 1), (z_step, 1, 0, 2, 1), (y_step, 1, 0, 1, 1), (y_step, 1, 1, 1, -1),
            (z_step, 1, 1, 1, -1), (z_step, 3, 0, 2, -1), (x_step, 2, 1, 0), (y_step, 1, 0, 1, -1),
            (z_step, 2, 1, 1, 1), (z_step, 2, 0, 1, 1), (z_step, 3, 1, 2, -1), (x_step, 2, 0, 0),
            (z_step, 1, 1, 2, 1), (y_step, 3, 0, 1, 1), (z_step, 2, 1, 1, -1), (z_step, 1, 0, 2, -1),
            (z_step, 2, 0, 1, -1), (y_begin, 2, 0), (z_step, 3, 1, 3, 1), (z_step, 3, 0, 3, 1),
            (y_step, 1, 1, 1, 1), (z_step, 1, 0, 3, 1), (y_step, 3, 1, 1, -1), (y_step, 3, 0, 1, -1),
            (z_step, 2, 0, 2, 1), (z_step, 3, 1, 3, -1), (z_step, 1, 1, 2, -1), (y_step, 3, 1, 1, 1),
            (y_begin, 2, 1), (z_step, 1, 1, 3, 1), (y_step, 1, 0, 2, 1), (z_step, 1, 0, 3, -1),
            (z_step, 2, 1, 2, -1), (z_step, 3, 0, 3, -1), (z_step, 2, 0, 2, -1), (z_step, 2, 1, 2, 1),
            (y_step, 3, 0, 2, 1), (y_step, 2, 0, 1, 1), (z_step, 3, 0, 4, 1), (z_step, 1, 0, 4, 1),
        ],
        [
            (z_step, 2, 0, 3, 1), (z_step, 1, 1, 3, -1),
        ],
        [
            (y_step, 1, 1, 2, 1), (z_step, 1, 1, 4, 1), (y_step, 3, 1, 2, 1), (z_step, 3, 1, 4, 1),
            (z_step, 2, 1, 3, 1), (y_step, 2, 0, 1, -1), (y_step, 2, 1, 1, 1),
        ],
        [
            (z_step, 2, 0, 3, -1), (z_step, 2, 0, 4, 1),
        ],
        [
            (z_step, 2, 1, 3, -1), (y_step, 2, 0, 2, 1), (y_step, 2, 1, 1, -1), (z_step, 2, 1, 4, 1),
            (y_step, 2, 1, 2, 1),
        ],
        [],
    ]

    def chunk(i, _):
        for t, steps in enumerate(plan):
            @pl.when(i == t)
            def _():
                for step, *rest in steps:
                    step(*rest)

        p, k = i // 2, i % 2
        score = jnp.dot(
            w[k], jnp.concatenate([hid[p, 0], hid[p, 1]], axis=1), preferred_element_type=F32)
        peak = jnp.max(score, axis=0, keepdims=True)
        t = (score - peak) * LOG2E
        e = jnp.exp2(t)
        total = jnp.sum(e, axis=0, keepdims=True)
        moment = jnp.sum(e * t, axis=0, keepdims=True)
        code = jnp.exp2(jnp.maximum(t, -FLOOR) * GAIN + BIAS).astype(BF16)
        for q in range(2):
            lanes = slice(128 * q, 128 * q + 128)
            codes[i, q] = code[:, lanes]
            for n, row in enumerate((peak, total, moment)):
                stats[i, q, n : n + 1] = row[:, lanes]
        cols_here = pl.ds(pl.multiple_of(COLS * x, 16), COLS)

        @pl.when(i == 0)
        def _():
            for q in range(2):
                got[c, q, cols_here] = codes[i, q]
                gstat[x, 2 * c + q] = stats[i, q]

        def send(i, k, piece, land, sems, n):
            for q in range(2):
                role = jnp.where(p == 0, 0, jnp.where(p == 3, 2, 1 + 2 * q))
                lg = jnp.where((p == 0) | (p == 3), q, p - 1)
                device = (at(z, y, jnp.where(k == 1, 1 - c, c)), lax.rem(x + role * sg + NX, NX))
                pltpu.make_async_remote_copy(
                    piece.at[i, q], land(lg), send_sem.at[n], sems.at[x, c, lg],
                    device_id=device, device_id_type=MESH,
                ).start()

        def send_stats(i, k):
            send(i, k, stats, lambda lg: gstat.at[x, 2 * c + lg], stat_sem, 3)

        def send_codes(i, k):
            send(i, k, codes, lambda lg: got.at[c, lg, cols_here], code_sem, 2)

        @pl.when(i > 0)
        def _():
            send_stats(i, k)

        @pl.when((i > 0) & (i < 6))
        def _():
            send_codes(i, k)

        @pl.when(i == 7)
        def _():
            send_codes(6, 0)
            send_codes(7, 1)

        return 0

    lax.fori_loop(0, 8, chunk, 0)

    def await_groups(ref_of, sem):
        for s in range(NX):
            for h in ((1 - c,) if s == 0 else (c, 1 - c)):
                for lg in range(2):
                    ref = ref_of(xto[s], h, lg)
                    pltpu.make_async_copy(ref, ref, sem.at[xto[s], h, lg]).wait()

    await_groups(lambda xs, h, lg: gstat.at[xs, 2 * h + lg], stat_sem)

    def combined(peaks, totals, moments):
        top = functools.reduce(jnp.maximum, peaks)
        total = moment = None
        for a, b, d in zip(peaks, totals, moments):
            low = (a - top) * LOG2E
            f = jnp.exp2(low)
            m, n = b * f, f * (d + low * b)
            total = m if total is None else total + m
            moment = n if moment is None else moment + n
        return top, total, moment

    def swap_start(mine, slots, place, peers, n):
        slots[place] = mine[...]
        for peer in peers:
            pltpu.make_async_remote_copy(
                mine, slots.at[place], rsend_sem.at[n], round_sem.at[n],
                device_id=peer, device_id_type=MESH,
            ).start()

    def swap_end(slots, n):
        seven = slots.at[pl.ds(0, 7)]
        pltpu.make_async_copy(seven, seven, round_sem.at[n]).wait()

    def await_codes(s):
        cols_from = pl.ds(pl.multiple_of(COLS * xto[s], 16), COLS)
        for h in ((1 - c,) if s == 0 else (c, 1 - c)):
            for lg in range(2):
                ref = got.at[h, lg, cols_from]
                pltpu.make_async_copy(ref, ref, code_sem.at[xto[s], h, lg]).wait()

    def decode(sources):
        for s in sources:
            await_codes(s)

        def one(group, _):
            for s in sources:
                cols_from = pl.ds(pl.multiple_of(COLS * xto[s], 16), COLS)
                sent = got[group // 2, group % 2, cols_from].astype(F32)
                keep[group, cols_from] = jnp.exp2((jnp.log2(sent) - BIAS) * (1.0 / GAIN))
            return 0
        lax.fori_loop(0, 4, one, 0)

    peaks = [gstat[k, :, 0, :] for k in range(NX)]
    top, total, moment = combined(
        peaks, [gstat[k, :, 1, :] for k in range(NX)], [gstat[k, :, 2, :] for k in range(NX)])
    yc = y * 2 + c
    for slots, place_at, peer_set, n in ((zpart, z, zpeers, 0), (ypart, yc, ypeers, 1)):
        part[n, 0] = top
        part[n, 1] = total
        part[n, 2] = moment
        swap_start(part.at[n], slots, place_at, peer_set, n)
        decode(((0, 1), (3,))[n])
        swap_end(slots, n)
        top, total, moment = combined(
            *([slots[k, n] for k in range(8)] for n in range(3)))

    eta = eta_ref[...]
    entropy = jnp.log(total) - moment / total * LN2
    limit = jnp.minimum(eta, jnp.sqrt(eta) * jnp.exp(-entropy))
    ent_ref[...] = entropy
    under = jnp.log2(total)
    for k in range(NX):
        cols[:, k, :] = jnp.exp2((peaks[k] - top) * LOG2E - under)
    cols[:, NX, :] = limit

    def weigh(group, sources):
        cut = cols[group, NX : NX + 1]
        mass = jnp.zeros((1, 128), F32)
        for s in sources:
            cols_from = pl.ds(pl.multiple_of(COLS * xto[s], 16), COLS)
            prob = keep[group, cols_from] * cols[group, pl.ds(xto[s], 1)]
            weight = jnp.maximum(prob - cut, 0.0)
            keep[group, cols_from] = weight
            mass = mass + jnp.sum(weight, axis=0, keepdims=True)
        kept[0, pl.ds(group, 1)] = kept[0, pl.ds(group, 1)] + mass

    for sources in ((0, 1, 3), (2,)):
        if sources == (2,):
            decode(sources)

        def weigh_group(group, _, sources=sources):
            weigh(group, sources)
            return 0
        lax.fori_loop(0, 4, weigh_group, 0)

    def finish(group, _):
        least = 0.001 * cols[group, NX : NX + 1]
        rows = pl.ds(pl.multiple_of(128 * group, 128), 128)
        for tile in range(OUT // 128):
            at_tile = slice(128 * tile, 128 * tile + 128)
            log_ref[rows, at_tile] = jnp.log(keep[group, at_tile] + least).T
        return 0

    for slots, place_at, peer_set, n in ((zkept, z, zpeers, 2), (ykept, yc, ypeers, 3)):
        swap_start(kept.at[n - 2], slots, place_at, peer_set, n)
        lax.fori_loop(2 * n - 4, 2 * n - 2, finish, 0)
        swap_end(slots, n)
        mass = slots[0]
        for k in range(1, 8):
            mass = mass + slots[k]
        if n == 2:
            kept[1] = mass
    lkm_ref[...] = jnp.log(mass)

    for n, ref in ((0, hid.at[pl.ds(0, 3)]), (2, codes.at[pl.ds(0, 7)]), (3, stats.at[pl.ds(0, 7)])):
        pltpu.make_async_copy(ref, ref, send_sem.at[n]).wait()
    for n, slots in enumerate((zpart, ypart, zkept, ykept)):
        seven = slots.at[pl.ds(0, 7)]
        pltpu.make_async_copy(seven, seven, rsend_sem.at[n]).wait()
    w_out.wait_send()


def write_out(log_ref, lkm_ref, ent_ref, out_hbm, ent_out, out, sem):
    copies = []
    for group in range(4):
        rows = slice(128 * group, 128 * group + 128)
        less = jnp.broadcast_to(lkm_ref[group : group + 1], (128, 128)).T
        for tile in range(OUT // 128):
            at_tile = slice(128 * tile, 128 * tile + 128)
            out[group, :, at_tile] = log_ref[rows, at_tile] - less
        copies.append(pltpu.make_async_copy(out.at[group], out_hbm.at[rows], sem.at[group]))
        copies[-1].start()
    ent_out[...] = ent_ref[...]
    for copy in copies:
        copy.wait()


def shards(hidden, head_weight, eta_level):
    dma = pltpu.SemaphoreType.DMA
    vmem = pltpu.VMEM
    logs, lkm, ent = pl.pallas_call(
        kernel,
        out_shape=(
            jax.ShapeDtypeStruct((ROWS, OUT), F32),
            jax.ShapeDtypeStruct((4, 128), F32),
            jax.ShapeDtypeStruct((4, 128), F32),
        ),
        in_specs=[
            pl.BlockSpec(memory_space=pltpu.HBM),
            pl.BlockSpec(memory_space=pltpu.HBM),
            pl.BlockSpec(memory_space=pltpu.HBM),
        ],
        out_specs=(
            pl.BlockSpec(memory_space=vmem),
            pl.BlockSpec(memory_space=vmem),
            pl.BlockSpec(memory_space=vmem),
        ),
        scratch_shapes=[
            vmem((4, 2, D, 128), BF16),
            vmem((2, COLS, D), BF16),
            vmem((4, 128), F32),
            vmem((8, 2, COLS, 128), BF16),
            vmem((8, 2, 8, 128), F32),
            vmem((2, 2, OUT, 128), BF16),
            vmem((NX, 4, 8, 128), F32),
            vmem((4, OUT, 128), F32),
            vmem((4, 8, 128), F32),
            vmem((2, 3, 4, 128), F32),
            vmem((8, 3, 4, 128), F32),
            vmem((8, 3, 4, 128), F32),
            vmem((2, 4, 128), F32),
            vmem((8, 4, 128), F32),
            vmem((8, 4, 128), F32),
            dma((4,)),
            dma((4,)),
            dma((1,)),
            dma((4, 2, 2)),
            dma((4, 2, 5, 2)),
            dma((4, 2, 3, 2)),
            dma((NX, 2, 2)),
            dma((NX, 2, 2)),
            dma((4,)),
            dma((4,)),
        ],
        compiler_params=pltpu.CompilerParams(
            collective_id=0, has_side_effects=True, vmem_limit_bytes=40 * 2**20),
        cost_estimate=pl.CostEstimate(
            flops=2 * ROWS * D * OUT, bytes_accessed=10 * 2**20, transcendentals=5 * ROWS * OUT),
        name="eta_filter",
    )(
        pltpu.with_memory_space_constraint(hidden.T, pltpu.HBM),
        pltpu.with_memory_space_constraint(head_weight.T, pltpu.HBM),
        pltpu.with_memory_space_constraint(eta_level.reshape(4, 128), pltpu.HBM),
    )
    filtered, entropy = pl.pallas_call(
        write_out,
        out_shape=(jax.ShapeDtypeStruct((ROWS, OUT), F32), jax.ShapeDtypeStruct((4, 128), F32)),
        in_specs=[pl.BlockSpec(memory_space=vmem)] * 3,
        out_specs=(pl.BlockSpec(memory_space=pltpu.HBM), pl.BlockSpec(memory_space=vmem)),
        scratch_shapes=[vmem((4, 128, OUT), F32), dma((4,))],
        compiler_params=pltpu.CompilerParams(vmem_limit_bytes=16 * 2**20),
        cost_estimate=pl.CostEstimate(flops=ROWS * OUT, bytes_accessed=4 * ROWS * OUT, transcendentals=0),
        name="write_out",
    )(pltpu.with_memory_space_constraint(logs, vmem), lkm, ent)
    return filtered, entropy.reshape(ROWS)


def solution(mesh):
    return jax.shard_map(
        shards,
        mesh=mesh,
        in_specs=(P("rows", None), P(None, ("vocab", "rows")), P("rows")),
        out_specs=(P("rows", "vocab"), P("rows")),
        check_vma=False,
    )
```

```python
import functools

import jax
import jax.numpy as jnp
from jax import lax
from jax.experimental import pallas as pl
from jax.experimental.pallas import tpu as pltpu
from jax.sharding import PartitionSpec as P

MESH = pl.DeviceIdType.MESH
F32 = jnp.float32
BF16 = jnp.bfloat16

NX, NY, NZ = 4, 4, 8
D = 2880
ROWS = 512
COLS = 416
OUT = NX * COLS
YPART = 432
ZPART = 144

LOG2E = 1.4426950408889634
LN2 = 0.6931471805599453
GAIN = 10.5
BIAS = 123.0
FLOOR = 23.5


def far_first(n):
    return sorted(range(1, n), key=lambda k: -min(k, n - k))


PLACE = {(1, 0): (1, 0), (3, 0): (1, 1), (1, 1): (2, 0), (3, 1): (2, 1), (2, 0): (3, 0), (2, 1): (3, 1)}


def kernel(
    hid_hbm, w_hbm, eta_hbm,
    log_ref, lkm_ref, ent_ref,
    hid, w, eta_ref, codes, stats, got, gstat, keep,
    cols, part, zpart, ypart, kept, zkept, ykept,
    load_sem, send_sem, w_sem, x_sem, z_sem, y_sem, code_sem, stat_sem, round_sem, rsend_sem,
):
    v = lax.axis_index("vocab")
    x = lax.axis_index("rows")
    z, y, c = v // 8, (v // 2) % 4, v % 2
    sg = 1 - 2 * c

    def at(z, y, c):
        return (z * NY + y) * 2 + c

    here = at(z, y, c)
    sibling = at(z, y, 1 - c)
    zto = [lax.rem(z + k, NZ) for k in range(NZ)]
    yto = [lax.rem(y + k, NY) for k in range(NY)]
    xto = [lax.rem(x + k, NX) for k in range(NX)]
    x_ahead, x_back = lax.rem(x + sg + NX, NX), lax.rem(x - sg + NX, NX)
    y_ahead, y_back = lax.rem(y + sg + NY, NY), lax.rem(y - sg + NY, NY)
    z_ahead, z_back = lax.rem(z + sg + NZ, NZ), lax.rem(z - sg + NZ, NZ)

    zpeers = [(at(zto[k], y, c), x) for k in far_first(NZ)]
    ypeers = [(at(z, yto[2], c), x)]
    ypeers += [(at(z, yto[k], 1 - c), x) for k in (2, 1, 3)]
    ypeers += [(at(z, yto[k], c), x) for k in (1, 3)] + [(sibling, x)]
    xpeers = [(d, xto[k]) for k in (2, 1, 3) for d in (here, sibling)]

    barrier = pltpu.get_barrier_semaphore()
    peers = zpeers + ypeers + xpeers
    for peer in peers:
        pl.semaphore_signal(barrier, 1, device_id=peer, device_id_type=MESH)

    def lanes_of(lg):
        return pl.ds(pl.multiple_of(256 * c + 128 * lg, 128), 128)

    own = [
        pltpu.make_async_copy(hid_hbm.at[:, lanes_of(lg)], hid.at[0, lg], load_sem.at[lg])
        for lg in range(2)
    ]
    own.append(pltpu.make_async_copy(w_hbm, w.at[0], load_sem.at[2]))
    own.append(pltpu.make_async_copy(eta_hbm, eta_ref, load_sem.at[3]))
    for copy in own:
        copy.start()
    part[...] = jnp.zeros_like(part)
    kept[...] = jnp.zeros_like(kept)
    pl.semaphore_wait(barrier, len(peers))

    def y_rows(j):
        return pl.ds(pl.multiple_of(YPART * j, 16), YPART)

    def z_rows(j):
        return pl.ds(pl.multiple_of(NY * YPART + ZPART * j, 16), ZPART)

    def hid_at(role, lg, rows):
        p, q = PLACE[role, lg]
        return hid.at[p, q, rows]

    def x_send(lg, along_z, ahead):
        rows = z_rows(z) if along_z else y_rows(y)
        role = 3 if ahead else 1
        pltpu.make_async_remote_copy(
            hid_hbm.at[rows, lanes_of(lg)], hid_at(role, lg, rows),
            send_sem.at[0], x_sem.at[role, lg, along_z],
            device_id=(here, x_ahead if ahead else x_back), device_id_type=MESH,
        ).start()

    x_send(1, 1, True)
    x_send(0, 1, True)
    x_send(1, 0, False)
    x_send(0, 1, False)
    w_out = pltpu.make_async_remote_copy(
        w_hbm, w.at[1], send_sem.at[1], w_sem.at[0], device_id=(sibling, x), device_id_type=MESH)
    w_out.start()
    x_send(1, 1, False)
    x_send(0, 0, False)
    x_send(0, 0, True)
    x_send(1, 0, True)

    def arrived(ref, sem):
        pltpu.make_async_copy(ref, ref, sem).wait()

    def pass_on(ref, sem, device):
        pltpu.make_async_remote_copy(
            ref, ref, send_sem.at[0], sem, device_id=device, device_id_type=MESH).start()

    def x_step(role, lg, along_z):
        rows = z_rows(z) if along_z else y_rows(y)
        ref = hid_at(role, lg, rows)
        arrived(ref, x_sem.at[role, lg, along_z])
        if role == (1 if along_z else 3):
            pltpu.make_async_remote_copy(
                ref, hid_at(2, lg, rows), send_sem.at[0], x_sem.at[2, lg, along_z],
                device_id=(here, x_back if along_z else x_ahead), device_id_type=MESH,
            ).start()

    def z_begin(role, lg):
        ref = hid_at(role, lg, z_rows(z))
        pass_on(ref, z_sem.at[role, lg, 1, 0], (at(z_ahead, y, c), x))
        pass_on(ref, z_sem.at[role, lg, 1, 1], (at(z_back, y, c), x))

    def z_step(role, lg, t, way):
        side = (1 - way) // 2
        ref = hid_at(role, lg, z_rows(lax.rem(z - way * t * sg + NZ, NZ)))
        arrived(ref, z_sem.at[role, lg, t, side])
        if t < (4, 3)[side]:
            pass_on(ref, z_sem.at[role, lg, t + 1, side], (at((z_ahead, z_back)[side], y, c), x))

    def y_begin(role, lg):
        ref = hid_at(role, lg, y_rows(y))
        pass_on(ref, y_sem.at[role, lg, 1, 0], (at(z, y_ahead, c), x))
        pass_on(ref, y_sem.at[role, lg, 1, 1], (at(z, y_back, c), x))

    def y_step(role, lg, t, way):
        side = (1 - way) // 2
        ref = hid_at(role, lg, y_rows(lax.rem(y - way * t * sg + NY, NY)))
        arrived(ref, y_sem.at[role, lg, t, side])
        if t < (2, 1)[side]:
            pass_on(ref, y_sem.at[role, lg, t + 1, side], (at(z, (y_ahead, y_back)[side], c), x))

    def own_here():
        for copy in own:
            copy.wait()

    plan = [
        [
            (own_here,),
        ],
        [
            (x_step, 3, 1, 1), (z_begin, 3, 1), (x_step, 3, 0, 1), (z_begin, 3, 0), (x_step, 1, 1, 0),
            (y_begin, 1, 1), (x_step, 1, 0, 1), (x_step, 1, 1, 1), (z_begin, 1, 0), (z_step, 3, 1, 1, 1),
            (x_step, 1, 0, 0), (y_begin, 1, 0), (z_step, 3, 0, 1, 1), (z_begin, 1, 1),
            (z_step, 3, 1, 1, -1), (x_step, 3, 0, 0), (y_begin, 3, 0), (z_step, 3, 0, 1, -1),
            (z_step, 1, 0, 1, 1), (x_step, 3, 1, 0), (x_step, 2, 0, 1), (z_begin, 2, 0), (x_step, 2, 1, 1),
            (z_step, 1, 0, 1, -1), (z_begin, 2, 1), (y_begin, 3, 1), (z_step, 3, 1, 2, 1),
            (w_out.wait_recv,), (z_step, 1, 1, 1, 1),
        ],
        [
            (z_step, 3, 0, 2, 1), (z_step, 1, 0, 2, 1), (y_step, 1, 0, 1, 1), (y_step, 1, 1, 1, -1),
            (z_step, 1, 1, 1, -1), (z_step, 3, 0, 2, -1), (x_step, 2, 1, 0), (y_step, 1, 0, 1, -1),
            (z_step, 2, 1, 1, 1), (z_step, 2, 0, 1, 1), (z_step, 3, 1, 2, -1), (x_step, 2, 0, 0),
            (z_step, 1, 1, 2, 1), (y_step, 3, 0, 1, 1), (z_step, 2, 1, 1, -1), (z_step, 1, 0, 2, -1),
            (z_step, 2, 0, 1, -1), (y_begin, 2, 0), (z_step, 3, 1, 3, 1), (z_step, 3, 0, 3, 1),
            (y_step, 1, 1, 1, 1), (z_step, 1, 0, 3, 1), (y_step, 3, 1, 1, -1), (y_step, 3, 0, 1, -1),
            (z_step, 2, 0, 2, 1), (z_step, 3, 1, 3, -1), (z_step, 1, 1, 2, -1), (y_step, 3, 1, 1, 1),
            (y_begin, 2, 1), (z_step, 1, 1, 3, 1), (y_step, 1, 0, 2, 1), (z_step, 1, 0, 3, -1),
            (z_step, 2, 1, 2, -1), (z_step, 3, 0, 3, -1), (z_step, 2, 0, 2, -1), (z_step, 2, 1, 2, 1),
            (y_step, 3, 0, 2, 1), (y_step, 2, 0, 1, 1), (z_step, 3, 0, 4, 1), (z_step, 1, 0, 4, 1),
        ],
        [
            (z_step, 2, 0, 3, 1), (z_step, 1, 1, 3, -1),
        ],
        [
            (y_step, 1, 1, 2, 1), (z_step, 1, 1, 4, 1), (y_step, 3, 1, 2, 1), (z_step, 3, 1, 4, 1),
            (z_step, 2, 1, 3, 1), (y_step, 2, 0, 1, -1), (y_step, 2, 1, 1, 1),
        ],
        [
            (z_step, 2, 0, 3, -1), (z_step, 2, 0, 4, 1),
        ],
        [
            (z_step, 2, 1, 3, -1), (y_step, 2, 0, 2, 1), (y_step, 2, 1, 1, -1), (z_step, 2, 1, 4, 1),
            (y_step, 2, 1, 2, 1),
        ],
        [],
    ]

    def chunk(i, _):
        for t, steps in enumerate(plan):
            @pl.when(i == t)
            def _():
                for step, *rest in steps:
                    step(*rest)

        p, k = i // 2, i % 2
        score = jnp.dot(
            w[k], jnp.concatenate([hid[p, 0], hid[p, 1]], axis=1), preferred_element_type=F32)
        peak = jnp.max(score, axis=0, keepdims=True)
        t = (score - peak) * LOG2E
        e = jnp.exp2(t)
        total = jnp.sum(e, axis=0, keepdims=True)
        moment = jnp.sum(e * t, axis=0, keepdims=True)
        code = jnp.exp2(jnp.maximum(t, -FLOOR) * GAIN + BIAS).astype(BF16)
        for q in range(2):
            lanes = slice(128 * q, 128 * q + 128)
            codes[i, q] = code[:, lanes]
            for n, row in enumerate((peak, total, moment)):
                stats[i, q, n : n + 1] = row[:, lanes]
        cols_here = pl.ds(pl.multiple_of(COLS * x, 16), COLS)

        @pl.when(i == 0)
        def _():
            for q in range(2):
                got[c, q, cols_here] = codes[i, q]
                gstat[x, 2 * c + q] = stats[i, q]

        def send(i, k, piece, land, sems, n):
            for q in range(2):
                role = jnp.where(p == 0, 0, jnp.where(p == 3, 2, 1 + 2 * q))
                lg = jnp.where((p == 0) | (p == 3), q, p - 1)
                device = (at(z, y, jnp.where(k == 1, 1 - c, c)), lax.rem(x + role * sg + NX, NX))
                pltpu.make_async_remote_copy(
                    piece.at[i, q], land(lg), send_sem.at[n], sems.at[x, c, lg],
                    device_id=device, device_id_type=MESH,
                ).start()

        def send_stats(i, k):
            send(i, k, stats, lambda lg: gstat.at[x, 2 * c + lg], stat_sem, 3)

        def send_codes(i, k):
            send(i, k, codes, lambda lg: got.at[c, lg, cols_here], code_sem, 2)

        @pl.when(i > 0)
        def _():
            send_stats(i, k)

        @pl.when((i > 0) & (i < 6))
        def _():
            send_codes(i, k)

        @pl.when(i == 7)
        def _():
            send_codes(6, 0)
            send_codes(7, 1)

        return 0

    lax.fori_loop(0, 8, chunk, 0)

    def await_groups(ref_of, sem):
        for s in range(NX):
            for h in ((1 - c,) if s == 0 else (c, 1 - c)):
                for lg in range(2):
                    ref = ref_of(xto[s], h, lg)
                    pltpu.make_async_copy(ref, ref, sem.at[xto[s], h, lg]).wait()

    await_groups(lambda xs, h, lg: gstat.at[xs, 2 * h + lg], stat_sem)

    def combined(peaks, totals, moments):
        top = functools.reduce(jnp.maximum, peaks)
        total = moment = None
        for a, b, d in zip(peaks, totals, moments):
            low = (a - top) * LOG2E
            f = jnp.exp2(low)
            m, n = b * f, f * (d + low * b)
            total = m if total is None else total + m
            moment = n if moment is None else moment + n
        return top, total, moment

    def swap_start(mine, slots, place, peers, n):
        slots[place] = mine[...]
        for peer in peers:
            pltpu.make_async_remote_copy(
                mine, slots.at[place], rsend_sem.at[n], round_sem.at[n],
                device_id=peer, device_id_type=MESH,
            ).start()

    def swap_end(slots, n):
        seven = slots.at[pl.ds(0, 7)]
        pltpu.make_async_copy(seven, seven, round_sem.at[n]).wait()

    peaks = [gstat[k, :, 0, :] for k in range(NX)]
    top, total, moment = combined(
        peaks, [gstat[k, :, 1, :] for k in range(NX)], [gstat[k, :, 2, :] for k in range(NX)])
    yc = y * 2 + c
    for slots, place_at, peer_set, n in ((zpart, z, zpeers, 0), (ypart, yc, ypeers, 1)):
        part[n, 0] = top
        part[n, 1] = total
        part[n, 2] = moment
        swap_start(part.at[n], slots, place_at, peer_set, n)
        swap_end(slots, n)
        top, total, moment = combined(
            *([slots[k, n] for k in range(8)] for n in range(3)))

    eta = eta_ref[...]
    entropy = jnp.log(total) - moment / total * LN2
    limit = jnp.minimum(eta, jnp.sqrt(eta) * jnp.exp(-entropy))
    ent_ref[...] = entropy
    under = jnp.log2(total) + BIAS / GAIN
    for k in range(NX):
        cols[:, k, :] = (peaks[k] - top) * LOG2E - under
    cols[:, NX, :] = limit

    def await_codes(s):
        cols_from = pl.ds(pl.multiple_of(COLS * xto[s], 16), COLS)
        for h in ((1 - c,) if s == 0 else (c, 1 - c)):
            for lg in range(2):
                ref = got.at[h, lg, cols_from]
                pltpu.make_async_copy(ref, ref, code_sem.at[xto[s], h, lg]).wait()

    def weigh(group, sources):
        cut = cols[group, NX : NX + 1]
        mass = jnp.zeros((1, 128), F32)
        for s in sources:
            cols_from = pl.ds(pl.multiple_of(COLS * xto[s], 16), COLS)
            sent = got[group // 2, group % 2, cols_from].astype(F32)
            prob = jnp.exp2(jnp.log2(sent) * (1.0 / GAIN) + cols[group, pl.ds(xto[s], 1)])
            weight = jnp.maximum(prob - cut, 0.0)
            keep[group, cols_from] = weight
            mass = mass + jnp.sum(weight, axis=0, keepdims=True)
        kept[0, pl.ds(group, 1)] = kept[0, pl.ds(group, 1)] + mass

    for sources in ((0, 1, 3), (2,)):
        for s in sources:
            await_codes(s)

        def weigh_group(group, _, sources=sources):
            weigh(group, sources)
            return 0
        lax.fori_loop(0, 4, weigh_group, 0)

    def finish(group, _):
        least = 0.001 * cols[group, NX : NX + 1]
        rows = pl.ds(pl.multiple_of(128 * group, 128), 128)
        for tile in range(OUT // 128):
            at_tile = slice(128 * tile, 128 * tile + 128)
            log_ref[rows, at_tile] = jnp.log(keep[group, at_tile] + least).T
        return 0

    for slots, place_at, peer_set, n in ((zkept, z, zpeers, 2), (ykept, yc, ypeers, 3)):
        swap_start(kept.at[n - 2], slots, place_at, peer_set, n)
        lax.fori_loop(2 * n - 4, 2 * n - 2, finish, 0)
        swap_end(slots, n)
        mass = slots[0]
        for k in range(1, 8):
            mass = mass + slots[k]
        if n == 2:
            kept[1] = mass
    lkm_ref[...] = jnp.log(mass)

    for n, ref in ((0, hid.at[pl.ds(0, 3)]), (2, codes.at[pl.ds(0, 7)]), (3, stats.at[pl.ds(0, 7)])):
        pltpu.make_async_copy(ref, ref, send_sem.at[n]).wait()
    for n, slots in enumerate((zpart, ypart, zkept, ykept)):
        seven = slots.at[pl.ds(0, 7)]
        pltpu.make_async_copy(seven, seven, rsend_sem.at[n]).wait()
    w_out.wait_send()


def write_out(log_ref, lkm_ref, ent_ref, out_hbm, ent_out, out, sem):
    copies = []
    for group in range(4):
        rows = slice(128 * group, 128 * group + 128)
        less = jnp.broadcast_to(lkm_ref[group : group + 1], (128, 128)).T
        for tile in range(OUT // 128):
            at_tile = slice(128 * tile, 128 * tile + 128)
            out[group, :, at_tile] = log_ref[rows, at_tile] - less
        copies.append(pltpu.make_async_copy(out.at[group], out_hbm.at[rows], sem.at[group]))
        copies[-1].start()
    ent_out[...] = ent_ref[...]
    for copy in copies:
        copy.wait()


def shards(hidden, head_weight, eta_level):
    dma = pltpu.SemaphoreType.DMA
    vmem = pltpu.VMEM
    logs, lkm, ent = pl.pallas_call(
        kernel,
        out_shape=(
            jax.ShapeDtypeStruct((ROWS, OUT), F32),
            jax.ShapeDtypeStruct((4, 128), F32),
            jax.ShapeDtypeStruct((4, 128), F32),
        ),
        in_specs=[
            pl.BlockSpec(memory_space=pltpu.HBM),
            pl.BlockSpec(memory_space=pltpu.HBM),
            pl.BlockSpec(memory_space=pltpu.HBM),
        ],
        out_specs=(
            pl.BlockSpec(memory_space=vmem),
            pl.BlockSpec(memory_space=vmem),
            pl.BlockSpec(memory_space=vmem),
        ),
        scratch_shapes=[
            vmem((4, 2, D, 128), BF16),
            vmem((2, COLS, D), BF16),
            vmem((4, 128), F32),
            vmem((8, 2, COLS, 128), BF16),
            vmem((8, 2, 8, 128), F32),
            vmem((2, 2, OUT, 128), BF16),
            vmem((NX, 4, 8, 128), F32),
            vmem((4, OUT, 128), F32),
            vmem((4, 8, 128), F32),
            vmem((2, 3, 4, 128), F32),
            vmem((8, 3, 4, 128), F32),
            vmem((8, 3, 4, 128), F32),
            vmem((2, 4, 128), F32),
            vmem((8, 4, 128), F32),
            vmem((8, 4, 128), F32),
            dma((4,)),
            dma((4,)),
            dma((1,)),
            dma((4, 2, 2)),
            dma((4, 2, 5, 2)),
            dma((4, 2, 3, 2)),
            dma((NX, 2, 2)),
            dma((NX, 2, 2)),
            dma((4,)),
            dma((4,)),
        ],
        compiler_params=pltpu.CompilerParams(
            collective_id=0, has_side_effects=True, vmem_limit_bytes=40 * 2**20),
        cost_estimate=pl.CostEstimate(
            flops=2 * ROWS * D * OUT, bytes_accessed=10 * 2**20, transcendentals=5 * ROWS * OUT),
        name="eta_filter",
    )(
        pltpu.with_memory_space_constraint(hidden.T, pltpu.HBM),
        pltpu.with_memory_space_constraint(head_weight.T, pltpu.HBM),
        pltpu.with_memory_space_constraint(eta_level.reshape(4, 128), pltpu.HBM),
    )
    filtered, entropy = pl.pallas_call(
        write_out,
        out_shape=(jax.ShapeDtypeStruct((ROWS, OUT), F32), jax.ShapeDtypeStruct((4, 128), F32)),
        in_specs=[pl.BlockSpec(memory_space=vmem)] * 3,
        out_specs=(pl.BlockSpec(memory_space=pltpu.HBM), pl.BlockSpec(memory_space=vmem)),
        scratch_shapes=[vmem((4, 128, OUT), F32), dma((4,))],
        compiler_params=pltpu.CompilerParams(vmem_limit_bytes=16 * 2**20),
        cost_estimate=pl.CostEstimate(flops=ROWS * OUT, bytes_accessed=4 * ROWS * OUT, transcendentals=0),
        name="write_out",
    )(pltpu.with_memory_space_constraint(logs, vmem), lkm, ent)
    return filtered, entropy.reshape(ROWS)


def solution(mesh):
    return jax.shard_map(
        shards,
        mesh=mesh,
        in_specs=(P("rows", None), P(None, ("vocab", "rows")), P("rows")),
        out_specs=(P("rows", "vocab"), P("rows")),
        check_vma=False,
    )
```

```python
import functools

import jax
import jax.numpy as jnp
from jax import lax
from jax.experimental import pallas as pl
from jax.experimental.pallas import tpu as pltpu
from jax.sharding import PartitionSpec as P

MESH = pl.DeviceIdType.MESH
F32 = jnp.float32
BF16 = jnp.bfloat16

NX, NY, NZ = 4, 4, 8
D = 2880
ROWS = 512
COLS = 416
OUT = NX * COLS
YPART = 432
ZPART = 144

LOG2E = 1.4426950408889634
LN2 = 0.6931471805599453
GAIN = 10.5
BIAS = 123.0
FLOOR = 23.5


def far_first(n):
    return sorted(range(1, n), key=lambda k: -min(k, n - k))


PLACE = {(1, 0): (1, 0), (3, 0): (1, 1), (1, 1): (2, 0), (3, 1): (2, 1), (2, 0): (3, 0), (2, 1): (3, 1)}


def kernel(
    hid_hbm, w_hbm, eta_hbm,
    log_ref, lkm_ref, ent_ref,
    hid, w, eta_ref, codes, stats, got, gstat, keep,
    cols, part, zpart, ypart, kept, zkept, ykept,
    load_sem, send_sem, w_sem, x_sem, z_sem, y_sem, code_sem, stat_sem, round_sem, rsend_sem,
):
    v = lax.axis_index("vocab")
    x = lax.axis_index("rows")
    z, y, c = v // 8, (v // 2) % 4, v % 2
    sg = 1 - 2 * c

    def at(z, y, c):
        return (z * NY + y) * 2 + c

    here = at(z, y, c)
    sibling = at(z, y, 1 - c)
    zto = [lax.rem(z + k, NZ) for k in range(NZ)]
    yto = [lax.rem(y + k, NY) for k in range(NY)]
    xto = [lax.rem(x + k, NX) for k in range(NX)]
    x_ahead, x_back = lax.rem(x + sg + NX, NX), lax.rem(x - sg + NX, NX)
    y_ahead, y_back = lax.rem(y + sg + NY, NY), lax.rem(y - sg + NY, NY)
    z_ahead, z_back = lax.rem(z + sg + NZ, NZ), lax.rem(z - sg + NZ, NZ)

    zpeers = [(at(zto[k], y, c), x) for k in far_first(NZ)]
    ypeers = [(at(z, yto[2], c), x)]
    ypeers += [(at(z, yto[k], 1 - c), x) for k in (2, 1, 3)]
    ypeers += [(at(z, yto[k], c), x) for k in (1, 3)] + [(sibling, x)]
    xpeers = [(d, xto[k]) for k in (2, 1, 3) for d in (here, sibling)]

    barrier = pltpu.get_barrier_semaphore()
    peers = zpeers + ypeers + xpeers
    for peer in peers:
        pl.semaphore_signal(barrier, 1, device_id=peer, device_id_type=MESH)

    def lanes_of(lg):
        return pl.ds(pl.multiple_of(256 * c + 128 * lg, 128), 128)

    own = [
        pltpu.make_async_copy(hid_hbm.at[:, lanes_of(lg)], hid.at[0, lg], load_sem.at[lg])
        for lg in range(2)
    ]
    own.append(pltpu.make_async_copy(w_hbm, w.at[0], load_sem.at[2]))
    own.append(pltpu.make_async_copy(eta_hbm, eta_ref, load_sem.at[3]))
    for copy in own:
        copy.start()
    part[...] = jnp.zeros_like(part)
    kept[...] = jnp.zeros_like(kept)
    pl.semaphore_wait(barrier, len(peers))

    def y_rows(j):
        return pl.ds(pl.multiple_of(YPART * j, 16), YPART)

    def z_rows(j):
        return pl.ds(pl.multiple_of(NY * YPART + ZPART * j, 16), ZPART)

    def hid_at(role, lg, rows):
        p, q = PLACE[role, lg]
        return hid.at[p, q, rows]

    def x_send(lg, along_z, ahead):
        rows = z_rows(z) if along_z else y_rows(y)
        role = 3 if ahead else 1
        pltpu.make_async_remote_copy(
            hid_hbm.at[rows, lanes_of(lg)], hid_at(role, lg, rows),
            send_sem.at[0], x_sem.at[role, lg, along_z],
            device_id=(here, x_ahead if ahead else x_back), device_id_type=MESH,
        ).start()

    x_send(1, 1, True)
    x_send(0, 1, True)
    x_send(1, 0, False)
    x_send(0, 1, False)
    w_out = pltpu.make_async_remote_copy(
        w_hbm, w.at[1], send_sem.at[1], w_sem.at[0], device_id=(sibling, x), device_id_type=MESH)
    w_out.start()
    x_send(1, 1, False)
    x_send(0, 0, False)
    x_send(0, 0, True)
    x_send(1, 0, True)

    def arrived(ref, sem):
        pltpu.make_async_copy(ref, ref, sem).wait()

    def pass_on(ref, sem, device):
        pltpu.make_async_remote_copy(
            ref, ref, send_sem.at[0], sem, device_id=device, device_id_type=MESH).start()

    def x_step(role, lg, along_z):
        rows = z_rows(z) if along_z else y_rows(y)
        ref = hid_at(role, lg, rows)
        arrived(ref, x_sem.at[role, lg, along_z])
        if role == (1 if along_z else 3):
            pltpu.make_async_remote_copy(
                ref, hid_at(2, lg, rows), send_sem.at[0], x_sem.at[2, lg, along_z],
                device_id=(here, x_back if along_z else x_ahead), device_id_type=MESH,
            ).start()

    def z_begin(role, lg):
        ref = hid_at(role, lg, z_rows(z))
        pass_on(ref, z_sem.at[role, lg, 1, 0], (at(z_ahead, y, c), x))
        pass_on(ref, z_sem.at[role, lg, 1, 1], (at(z_back, y, c), x))

    def z_step(role, lg, t, way):
        side = (1 - way) // 2
        ref = hid_at(role, lg, z_rows(lax.rem(z - way * t * sg + NZ, NZ)))
        arrived(ref, z_sem.at[role, lg, t, side])
        if t < (4, 3)[side]:
            pass_on(ref, z_sem.at[role, lg, t + 1, side], (at((z_ahead, z_back)[side], y, c), x))

    def y_begin(role, lg):
        ref = hid_at(role, lg, y_rows(y))
        pass_on(ref, y_sem.at[role, lg, 1, 0], (at(z, y_ahead, c), x))
        pass_on(ref, y_sem.at[role, lg, 1, 1], (at(z, y_back, c), x))

    def y_step(role, lg, t, way):
        side = (1 - way) // 2
        ref = hid_at(role, lg, y_rows(lax.rem(y - way * t * sg + NY, NY)))
        arrived(ref, y_sem.at[role, lg, t, side])
        if t < (2, 1)[side]:
            pass_on(ref, y_sem.at[role, lg, t + 1, side], (at(z, (y_ahead, y_back)[side], c), x))

    def own_here():
        for copy in own:
            copy.wait()

    plan = [
        [
            (own_here,),
        ],
        [
            (x_step, 3, 1, 1), (z_begin, 3, 1), (x_step, 3, 0, 1), (z_begin, 3, 0), (x_step, 1, 1, 0),
            (y_begin, 1, 1), (x_step, 1, 0, 1), (x_step, 1, 1, 1), (z_begin, 1, 0), (z_step, 3, 1, 1, 1),
            (x_step, 1, 0, 0), (y_begin, 1, 0), (z_step, 3, 0, 1, 1), (z_begin, 1, 1),
            (z_step, 3, 1, 1, -1), (x_step, 3, 0, 0), (y_begin, 3, 0), (z_step, 3, 0, 1, -1),
            (z_step, 1, 0, 1, 1), (x_step, 3, 1, 0), (x_step, 2, 0, 1), (z_begin, 2, 0), (x_step, 2, 1, 1),
            (z_step, 1, 0, 1, -1), (z_begin, 2, 1), (y_begin, 3, 1), (z_step, 3, 1, 2, 1),
            (w_out.wait_recv,), (z_step, 1, 1, 1, 1),
        ],
        [
            (z_step, 3, 0, 2, 1), (z_step, 1, 0, 2, 1), (y_step, 1, 0, 1, 1), (y_step, 1, 1, 1, -1),
            (z_step, 1, 1, 1, -1), (z_step, 3, 0, 2, -1), (x_step, 2, 1, 0), (y_step, 1, 0, 1, -1),
            (z_step, 2, 1, 1, 1), (z_step, 2, 0, 1, 1), (z_step, 3, 1, 2, -1), (x_step, 2, 0, 0),
            (z_step, 1, 1, 2, 1), (y_step, 3, 0, 1, 1), (z_step, 2, 1, 1, -1), (z_step, 1, 0, 2, -1),
            (z_step, 2, 0, 1, -1), (y_begin, 2, 0), (z_step, 3, 1, 3, 1), (z_step, 3, 0, 3, 1),
            (y_step, 1, 1, 1, 1), (z_step, 1, 0, 3, 1), (y_step, 3, 1, 1, -1), (y_step, 3, 0, 1, -1),
            (z_step, 2, 0, 2, 1), (z_step, 3, 1, 3, -1), (z_step, 1, 1, 2, -1), (y_step, 3, 1, 1, 1),
            (y_begin, 2, 1), (z_step, 1, 1, 3, 1), (y_step, 1, 0, 2, 1), (z_step, 1, 0, 3, -1),
            (z_step, 2, 1, 2, -1), (z_step, 3, 0, 3, -1), (z_step, 2, 0, 2, -1), (z_step, 2, 1, 2, 1),
            (y_step, 3, 0, 2, 1), (y_step, 2, 0, 1, 1), (z_step, 3, 0, 4, 1), (z_step, 1, 0, 4, 1),
        ],
        [
            (z_step, 2, 0, 3, 1), (z_step, 1, 1, 3, -1),
        ],
        [
            (y_step, 1, 1, 2, 1), (z_step, 1, 1, 4, 1), (y_step, 3, 1, 2, 1), (z_step, 3, 1, 4, 1),
            (z_step, 2, 1, 3, 1), (y_step, 2, 0, 1, -1), (y_step, 2, 1, 1, 1),
        ],
        [
            (z_step, 2, 0, 3, -1), (z_step, 2, 0, 4, 1),
        ],
        [
            (z_step, 2, 1, 3, -1), (y_step, 2, 0, 2, 1), (y_step, 2, 1, 1, -1), (z_step, 2, 1, 4, 1),
            (y_step, 2, 1, 2, 1),
        ],
        [],
    ]

    def chunk(i, _):
        for t, steps in enumerate(plan):
            @pl.when(i == t)
            def _():
                for step, *rest in steps:
                    step(*rest)

        p, k = i // 2, i % 2
        score = jnp.dot(
            w[k], jnp.concatenate([hid[p, 0], hid[p, 1]], axis=1), preferred_element_type=F32)
        peak = jnp.max(score, axis=0, keepdims=True)
        t = (score - peak) * LOG2E
        e = jnp.exp2(t)
        total = jnp.sum(e, axis=0, keepdims=True)
        moment = jnp.sum(e * t, axis=0, keepdims=True)
        code = jnp.exp2(jnp.maximum(t, -FLOOR) * GAIN + BIAS).astype(BF16)
        for q in range(2):
            lanes = slice(128 * q, 128 * q + 128)
            codes[i, q] = code[:, lanes]
            for n, row in enumerate((peak, total, moment)):
                stats[i, q, n : n + 1] = row[:, lanes]
        cols_here = pl.ds(pl.multiple_of(COLS * x, 16), COLS)

        @pl.when(i == 0)
        def _():
            for q in range(2):
                got[c, q, cols_here] = codes[i, q]
                gstat[x, 2 * c + q] = stats[i, q]

        def send(i, k, piece, land, sems, n):
            for q in range(2):
                role = jnp.where(p == 0, 0, jnp.where(p == 3, 2, 1 + 2 * q))
                lg = jnp.where((p == 0) | (p == 3), q, p - 1)
                device = (at(z, y, jnp.where(k == 1, 1 - c, c)), lax.rem(x + role * sg + NX, NX))
                pltpu.make_async_remote_copy(
                    piece.at[i, q], land(lg), send_sem.at[n], sems.at[x, c, lg],
                    device_id=device, device_id_type=MESH,
                ).start()

        def send_stats(i, k):
            send(i, k, stats, lambda lg: gstat.at[x, 2 * c + lg], stat_sem, 3)

        def send_codes(i, k):
            send(i, k, codes, lambda lg: got.at[c, lg, cols_here], code_sem, 2)

        @pl.when(i > 0)
        def _():
            send_stats(i, k)

        @pl.when((i > 0) & (i < 6))
        def _():
            send_codes(i, k)

        @pl.when(i == 7)
        def _():
            send_codes(6, 0)
            send_codes(7, 1)

        return 0

    lax.fori_loop(0, 8, chunk, 0)

    def await_groups(ref_of, sem):
        for s in range(NX):
            for h in ((1 - c,) if s == 0 else (c, 1 - c)):
                for lg in range(2):
                    ref = ref_of(xto[s], h, lg)
                    pltpu.make_async_copy(ref, ref, sem.at[xto[s], h, lg]).wait()

    await_groups(lambda xs, h, lg: gstat.at[xs, 2 * h + lg], stat_sem)

    def combined(peaks, totals, moments):
        top = functools.reduce(jnp.maximum, peaks)
        total = moment = None
        for a, b, d in zip(peaks, totals, moments):
            low = (a - top) * LOG2E
            f = jnp.exp2(low)
            m, n = b * f, f * (d + low * b)
            total = m if total is None else total + m
            moment = n if moment is None else moment + n
        return top, total, moment

    def swap_start(mine, slots, place, peers, n):
        slots[place] = mine[...]
        for peer in peers:
            pltpu.make_async_remote_copy(
                mine, slots.at[place], rsend_sem.at[n], round_sem.at[n],
                device_id=peer, device_id_type=MESH,
            ).start()

    def swap_end(slots, n):
        seven = slots.at[pl.ds(0, 7)]
        pltpu.make_async_copy(seven, seven, round_sem.at[n]).wait()

    peaks = [gstat[k, :, 0, :] for k in range(NX)]
    top, total, moment = combined(
        peaks, [gstat[k, :, 1, :] for k in range(NX)], [gstat[k, :, 2, :] for k in range(NX)])
    yc = y * 2 + c
    for slots, place_at, peer_set, n in ((zpart, z, zpeers, 0), (ypart, yc, ypeers, 1)):
        part[n, 0] = top
        part[n, 1] = total
        part[n, 2] = moment
        swap_start(part.at[n], slots, place_at, peer_set, n)
        swap_end(slots, n)
        top, total, moment = combined(
            *([slots[k, n] for k in range(8)] for n in range(3)))

    eta = eta_ref[...]
    entropy = jnp.log(total) - moment / total * LN2
    limit = jnp.minimum(eta, jnp.sqrt(eta) * jnp.exp(-entropy))
    ent_ref[...] = entropy
    under = jnp.log2(total) + BIAS / GAIN
    for k in range(NX):
        cols[:, k, :] = (peaks[k] - top) * LOG2E - under
    cols[:, NX, :] = limit

    def await_codes(s):
        cols_from = pl.ds(pl.multiple_of(COLS * xto[s], 16), COLS)
        for h in ((1 - c,) if s == 0 else (c, 1 - c)):
            for lg in range(2):
                ref = got.at[h, lg, cols_from]
                pltpu.make_async_copy(ref, ref, code_sem.at[xto[s], h, lg]).wait()

    def weigh(group, sources):
        cut = cols[group, NX : NX + 1]
        mass = jnp.zeros((1, 128), F32)
        for s in sources:
            cols_from = pl.ds(pl.multiple_of(COLS * xto[s], 16), COLS)
            sent = got[group // 2, group % 2, cols_from].astype(F32)
            prob = jnp.exp2(jnp.log2(sent) * (1.0 / GAIN) + cols[group, pl.ds(xto[s], 1)])
            weight = jnp.maximum(prob - cut, 0.0)
            keep[group, cols_from] = weight
            mass = mass + jnp.sum(weight, axis=0, keepdims=True)
        kept[0, pl.ds(group, 1)] = kept[0, pl.ds(group, 1)] + mass

    for sources in ((0, 1, 3), (2,)):
        for s in sources:
            await_codes(s)

        def weigh_group(group, _, sources=sources):
            weigh(group, sources)
            return 0
        lax.fori_loop(0, 4, weigh_group, 0)

    def finish(group, _):
        least = 0.001 * cols[group, NX : NX + 1]
        rows = pl.ds(pl.multiple_of(128 * group, 128), 128)
        for tile in range(OUT // 128):
            at_tile = slice(128 * tile, 128 * tile + 128)
            log_ref[rows, at_tile] = jnp.log(keep[group, at_tile] + least).T
        return 0

    for slots, place_at, peer_set, n in ((zkept, z, zpeers, 2), (ykept, yc, ypeers, 3)):
        swap_start(kept.at[n - 2], slots, place_at, peer_set, n)
        lax.fori_loop(2 * n - 4, 2 * n - 2, finish, 0)
        swap_end(slots, n)
        mass = slots[0]
        for k in range(1, 8):
            mass = mass + slots[k]
        if n == 2:
            kept[1] = mass
    lkm_ref[...] = jnp.log(mass)

    for n, ref in ((0, hid.at[pl.ds(0, 3)]), (2, codes.at[pl.ds(0, 7)]), (3, stats.at[pl.ds(0, 7)])):
        pltpu.make_async_copy(ref, ref, send_sem.at[n]).wait()
    for n, slots in enumerate((zpart, ypart, zkept, ykept)):
        seven = slots.at[pl.ds(0, 7)]
        pltpu.make_async_copy(seven, seven, rsend_sem.at[n]).wait()
    w_out.wait_send()


def write_out(log_ref, lkm_ref, ent_ref, out_hbm, ent_hbm, out, sem):
    copies = [pltpu.make_async_copy(ent_ref, ent_hbm, sem.at[4])]
    copies[0].start()
    for group in range(4):
        rows = slice(128 * group, 128 * group + 128)
        less = jnp.broadcast_to(lkm_ref[group : group + 1], (128, 128)).T
        for tile in range(OUT // 128):
            at_tile = slice(128 * tile, 128 * tile + 128)
            out[group, :, at_tile] = log_ref[rows, at_tile] - less
        copies.append(pltpu.make_async_copy(out.at[group], out_hbm.at[rows], sem.at[group]))
        copies[-1].start()
    for copy in copies:
        copy.wait()


def shards(hidden, head_weight, eta_level):
    dma = pltpu.SemaphoreType.DMA
    vmem = pltpu.VMEM
    logs, lkm, ent = pl.pallas_call(
        kernel,
        out_shape=(
            jax.ShapeDtypeStruct((ROWS, OUT), F32),
            jax.ShapeDtypeStruct((4, 128), F32),
            jax.ShapeDtypeStruct((4, 128), F32),
        ),
        in_specs=[
            pl.BlockSpec(memory_space=pltpu.HBM),
            pl.BlockSpec(memory_space=pltpu.HBM),
            pl.BlockSpec(memory_space=pltpu.HBM),
        ],
        out_specs=(
            pl.BlockSpec(memory_space=vmem),
            pl.BlockSpec(memory_space=vmem),
            pl.BlockSpec(memory_space=vmem),
        ),
        scratch_shapes=[
            vmem((4, 2, D, 128), BF16),
            vmem((2, COLS, D), BF16),
            vmem((4, 128), F32),
            vmem((8, 2, COLS, 128), BF16),
            vmem((8, 2, 8, 128), F32),
            vmem((2, 2, OUT, 128), BF16),
            vmem((NX, 4, 8, 128), F32),
            vmem((4, OUT, 128), F32),
            vmem((4, 8, 128), F32),
            vmem((2, 3, 4, 128), F32),
            vmem((8, 3, 4, 128), F32),
            vmem((8, 3, 4, 128), F32),
            vmem((2, 4, 128), F32),
            vmem((8, 4, 128), F32),
            vmem((8, 4, 128), F32),
            dma((4,)),
            dma((4,)),
            dma((1,)),
            dma((4, 2, 2)),
            dma((4, 2, 5, 2)),
            dma((4, 2, 3, 2)),
            dma((NX, 2, 2)),
            dma((NX, 2, 2)),
            dma((4,)),
            dma((4,)),
        ],
        compiler_params=pltpu.CompilerParams(
            collective_id=0, has_side_effects=True, vmem_limit_bytes=40 * 2**20),
        cost_estimate=pl.CostEstimate(
            flops=2 * ROWS * D * OUT, bytes_accessed=10 * 2**20, transcendentals=5 * ROWS * OUT),
        name="eta_filter",
    )(
        pltpu.with_memory_space_constraint(hidden.T, pltpu.HBM),
        pltpu.with_memory_space_constraint(head_weight.T, pltpu.HBM),
        pltpu.with_memory_space_constraint(eta_level.reshape(4, 128), pltpu.HBM),
    )
    filtered, entropy = pl.pallas_call(
        write_out,
        out_shape=(jax.ShapeDtypeStruct((ROWS, OUT), F32), jax.ShapeDtypeStruct((4, 128), F32)),
        in_specs=[pl.BlockSpec(memory_space=vmem)] * 3,
        out_specs=(pl.BlockSpec(memory_space=pltpu.HBM), pl.BlockSpec(memory_space=pltpu.HBM)),
        scratch_shapes=[vmem((4, 128, OUT), F32), dma((5,))],
        compiler_params=pltpu.CompilerParams(vmem_limit_bytes=16 * 2**20),
        cost_estimate=pl.CostEstimate(flops=ROWS * OUT, bytes_accessed=4 * ROWS * OUT, transcendentals=0),
        name="write_out",
    )(pltpu.with_memory_space_constraint(logs, vmem), lkm, ent)
    return filtered, entropy.reshape(ROWS)


def solution(mesh):
    return jax.shard_map(
        shards,
        mesh=mesh,
        in_specs=(P("rows", None), P(None, ("vocab", "rows")), P("rows")),
        out_specs=(P("rows", "vocab"), P("rows")),
        check_vma=False,
    )
```
